32 devices in a mesh: groups: 2 (over y), pairs: 4 (over z), sub: 2 (over x), rep: 2 (over core).
Axes of the slice: x: 2, y: 2, z: 4, core: 2. Of those that a mesh axis runs over, the one named last changes fastest.
Arguments:
- integrals: bfloat16 [384, 128, 1024], P(('groups', 'pairs'), 'sub'), parts along dimension 0, may hold values from -0.21875 to 0.21875
- density: bfloat16 [384, 32, 1024], P(('groups', 'pairs'), 'rep'), parts along dimension 0, may hold values from -6 to 6
- block_owner: int32 [384], P(('groups', 'pairs')), parts along dimension 0, may hold values from 0 to 3, as said below
Outputs:
- coulomb: float32 [384, 32, 1024], P(('groups', 'pairs'), 'rep', 'sub'), parts along dimension 0
The draws below stay inside these ranges and needn't reach their ends.
There are 2 independent parts, one for each index of `groups`. The reference program is written for one: setup_inputs(seed, part) draws one part's arguments, and reference() takes and returns one part's arrays. A program takes and returns all parts, laid end to end along the dimension named above; each array names one. Nothing has to cross between parts.
Inputs may be any that keep to these rules, and one draw needn't show every extreme that they name: Block k sits in the integral slots of pair owner block_owner[k]; in the rows of one device no owner is named more than 24 times and some owner exactly 24 times; over all rows every owner is named exactly 48 times.
All inputs are finite; a program needn't handle non-finite values.
Results may differ from the reference program's by a relative error of at most 0.0029.
Values may be sent and summed in bfloat16 or wider, within the bound.
A program may use at most 64 MiB of HBM per device.

```python
import jax
import jax.numpy as jnp
import numpy as np
from jax import lax

P_SIZE = 128
NDENS = 32
BLK_DEV = 48
BB = 1024
NBLK = 192
CAP = 24
N_PAIRS = 4


def draw_block_owner(key, part):
    key = jax.random.fold_in(key, 11)
    cycle_values = [CAP, max(1, CAP // 2), max(1, CAP - 1), max(1, CAP // 4)]
    chosen = []
    remain = BLK_DEV
    counter = 0
    while remain > 0:
        amount = min(cycle_values[counter % 4], remain)
        chosen.append(amount)
        remain = remain - amount
        counter = counter + 1
    pattern = np.zeros(N_PAIRS, np.int32)
    pattern[:len(chosen)] = np.array(chosen, np.int32)
    key_first, key_second = jax.random.split(key)
    ordering = jax.random.permutation(key_first, N_PAIRS)
    spread = jnp.asarray(pattern)[ordering]
    sources = jnp.arange(N_PAIRS, dtype=jnp.int32)
    shifted = (sources[None, :] - sources[:, None]) % N_PAIRS
    counts = spread[shifted]
    finish = jnp.cumsum(counts, axis=1)
    local_ids = jnp.arange(BLK_DEV, dtype=jnp.int32)
    targets = jnp.sum((finish[:, None, :] <= local_ids[None, :, None]).astype(jnp.int32), axis=2)
    row_keys = jax.random.split(key_second, N_PAIRS)
    shuffled = jax.vmap(lambda one_key, one_row: jax.random.permutation(one_key, one_row))(row_keys, targets)
    return shuffled.reshape(-1).astype(jnp.int32)


def shard_levels(own_key, extent, cuts, low, high):
    factor_of = 1.0
    for position, blocks in cuts:
        heights = jax.random.uniform(jax.random.fold_in(jax.random.fold_in(own_key, 6), position), (blocks,), jnp.float32, low / len(cuts), high / len(cuts))
        factor_of = factor_of * jnp.repeat(jnp.exp(heights), extent[position] // blocks).reshape((-1,) + (1,) * (len(extent) - 1 - position))
    return factor_of


def noise(key, dims, deviation, limit, cuts=(), kind=jnp.bfloat16):
    gain = shard_levels(key, dims, cuts, -0.22, 0.18) if cuts else 1.0
    drawn = jax.random.normal(key, dims, jnp.float32) * deviation * gain
    return jnp.minimum(jnp.maximum(drawn, -limit), limit).astype(kind)


def setup_inputs(seed: int = 0, part: int = 0) -> dict:
    splits = jax.random.split(jax.random.key(seed), 4)
    own_keys = jax.random.split(jax.random.fold_in(splits[3], part), 4)
    return {
        "integrals": noise(own_keys[0], (NBLK, P_SIZE, BB), ((P_SIZE * NBLK * BB) ** -0.25), 0.21875, ((0, 4), (1, 2))),
        "density": noise(own_keys[1], (NBLK, NDENS, BB), 1.0, 6.0, ((0, 4), (1, 2))),
        "block_owner": draw_block_owner(jax.random.fold_in(jax.random.fold_in(splits[3], part), 71), part),
    }


def slot_index(block_owner):
    sources = jnp.arange(NBLK, dtype=jnp.int32) // BLK_DEV
    pairkey = sources * N_PAIRS + block_owner
    positions = jnp.arange(NBLK, dtype=jnp.int32)
    earlier = positions[None, :] < positions[:, None]
    same_pair = pairkey[None, :] == pairkey[:, None]
    rank_in = jnp.sum((same_pair & earlier).astype(jnp.int32), axis=1)
    cells = jnp.zeros((N_PAIRS * N_PAIRS,), jnp.int32).at[pairkey].add(1).reshape(N_PAIRS, N_PAIRS)
    preceding = jnp.cumsum(cells, axis=0) - cells
    return (block_owner * BLK_DEV + preceding[sources, block_owner] + rank_in).astype(jnp.int32)


def reference(integrals, density, block_owner):
    slots = slot_index(block_owner)
    ordered = jnp.zeros_like(density).at[slots].set(density)
    batches = NBLK // BLK_DEV
    int_groups = integrals.reshape(batches, BLK_DEV, P_SIZE, BB)
    den_groups = ordered.reshape(batches, BLK_DEV, NDENS, BB)

    def accumulate(total, pieces):
        left, right = pieces
        return total + jnp.einsum("jpx,jdx->pd", left.astype(jnp.float32), right.astype(jnp.float32)), None

    fitted, _ = lax.scan(accumulate, jnp.zeros((P_SIZE, NDENS), jnp.float32), (int_groups, den_groups))
    fitted_half = lax.optimization_barrier(fitted.astype(jnp.bfloat16)).astype(jnp.float32)

    def project(group):
        return jnp.einsum("pd,jpx->jdx", fitted_half, group.astype(jnp.float32))

    by_slot = lax.map(project, int_groups).reshape(NBLK, NDENS, BB)
    return by_slot[slots]
```

```python
import jax
import jax.numpy as jnp
from jax import lax
from jax.sharding import PartitionSpec as P


def on_device(integrals, density, block_owner):
    npairs = lax.axis_size("pairs")
    nsub = lax.axis_size("sub")
    blocks = density.shape[0]
    dens_dev = density.shape[1]
    width = density.shape[2] // nsub
    capacity = 2 * blocks // npairs
    integrals = lax.all_to_all(integrals, "sub", split_axis=2, concat_axis=1, tiled=True)
    density = lax.dynamic_slice_in_dim(density, lax.axis_index("sub") * width, width, axis=2)
    peer_ids = jnp.arange(npairs, dtype=jnp.int32)
    onehot = (block_owner[:, None] == peer_ids[None, :]).astype(jnp.int32)
    before = jnp.cumsum(onehot, axis=0) - onehot
    rank_in = jnp.sum(before * onehot, axis=1)
    outgoing = block_owner * capacity + rank_in
    buffer_ids = jnp.arange(npairs * capacity, dtype=jnp.int32)
    matches = (outgoing[None, :] == buffer_ids[:, None]).astype(jnp.int32)
    source_ids = jnp.sum(matches * jnp.arange(blocks, dtype=jnp.int32)[None, :], axis=1)
    packed = density[source_ids].reshape(npairs, capacity, dens_dev, width)
    arrived = lax.all_to_all(packed, "pairs", split_axis=0, concat_axis=0, tiled=True)
    sent = jnp.sum(onehot, axis=0)
    counts = lax.all_to_all(sent, "pairs", split_axis=0, concat_axis=0, tiled=True)
    finish = jnp.cumsum(counts)
    starts = finish - counts
    slot_ids = jnp.arange(blocks, dtype=jnp.int32)
    anchor = jnp.sum((finish[None, :] <= slot_ids[:, None]).astype(jnp.int32), axis=1)
    anchor_onehot = (anchor[:, None] == peer_ids[None, :]).astype(jnp.int32)
    offsets = slot_ids - jnp.sum(anchor_onehot * starts[None, :], axis=1)
    places = anchor * capacity + offsets
    slot_density = arrived.reshape(npairs * capacity, dens_dev, width)[places]
    partial_fit = jnp.einsum(
        "jpx,jdx->pd", integrals, slot_density, preferred_element_type=jnp.float32
    )
    fitted = lax.psum(partial_fit, ("pairs", "sub")).astype(jnp.bfloat16)
    slot_coulomb = jnp.einsum(
        "pd,jpx->jdx", fitted, integrals, preferred_element_type=jnp.float32
    ).astype(jnp.bfloat16)
    return_index = jnp.clip(
        starts[:, None] + jnp.arange(capacity, dtype=jnp.int32)[None, :], 0, blocks - 1
    ).reshape(-1)
    kept = slot_coulomb[return_index].reshape(npairs, capacity, dens_dev, width)
    homeward = lax.all_to_all(kept, "pairs", split_axis=0, concat_axis=0, tiled=True)
    coulomb = homeward.reshape(npairs * capacity, dens_dev, width)[outgoing]
    return coulomb.astype(jnp.float32)


def solution(mesh):
    in_specs = (
        P(("groups", "pairs"), "sub", None),
        P(("groups", "pairs"), "rep", None),
        P(("groups", "pairs")),
    )
    out_specs = P(("groups", "pairs"), "rep", "sub")
    return jax.shard_map(
        on_device, mesh=mesh, in_specs=in_specs, out_specs=out_specs, check_vma=False
    )
```

```python
import functools

import jax
import jax.numpy as jnp
from jax import lax
from jax.experimental import pallas as pl
from jax.experimental.pallas import tpu as pltpu
from jax.sharding import PartitionSpec as P

MESH = pl.DeviceIdType.MESH


def divisor(total, choices):
    for c in choices:
        if total % c == 0:
            return c
    return 1


def exchange(
    npairs,
    nsub,
    nrep,
    chunks,
    src_ref,
    out_ids_ref,
    counts_ref,
    integrals_ref,
    density_ref,
    out_ref,
    ints,
    den,
    pack,
    arrived,
    ret,
    homeward,
    counts_all,
    counts_smem,
    starts_smem,
    places_smem,
    fit_plane,
    fit_pairs,
    local_sem,
    own_sem,
    ints_send,
    ints_recv,
    den_send,
    den_recv,
    ret_send,
    ret_recv,
    cnt_send,
    cnt_recv,
    plane_send,
    plane_recv,
    pairs_send,
    pairs_recv,
):
    me = lax.axis_index("pairs")
    sub = lax.axis_index("sub")
    rep = lax.axis_index("rep")
    blocks, dens, _ = density_ref.shape
    xq = ints.shape[3]
    cap = arrived.shape[1] // npairs
    step = blocks // chunks

    def device(pair, s, r):
        return {"pairs": pair, "sub": s, "rep": r}

    def quarter(s, r):
        return pl.ds(pl.multiple_of((s * nrep + r) * xq, 128), xq)

    den_copy = pltpu.make_async_copy(
        density_ref.at[:, :, pl.ds(pl.multiple_of(sub * (nrep * xq), 128), nrep * xq)],
        den,
        local_sem,
    )
    den_copy.start()
    own_copy = pltpu.make_async_copy(
        integrals_ref.at[:, :, quarter(sub, rep)], ints.at[sub], own_sem
    )
    own_copy.start()

    pair_order = [lax.rem(me + npairs // 2 + i, npairs) for i in range(npairs - npairs // 2)] + [
        lax.rem(me + i, npairs) for i in range(1, npairs // 2)
    ]
    pair_peers = pair_order
    sub_peers = [lax.rem(sub + i, nsub) for i in range(1, nsub)]
    rep_peers = [lax.rem(rep + i, nrep) for i in range(1, nrep)]
    plane_peers = (
        [(sub, r) for r in rep_peers]
        + [(s, rep) for s in sub_peers]
        + [(s, r) for s in sub_peers for r in rep_peers]
    )

    barrier = pltpu.get_barrier_semaphore()
    greeted = 0
    for pair in pair_peers:
        for r in [rep] + rep_peers:
            pl.semaphore_signal(
                barrier, inc=1, device_id=device(pair, sub, r), device_id_type=MESH
            )
            greeted += 1
    for s, r in plane_peers:
        pl.semaphore_signal(barrier, inc=1, device_id=device(me, s, r), device_id_type=MESH)
        greeted += 1
    pl.semaphore_wait(barrier, greeted)

    def ints_copy(s, c, slot):
        return pltpu.make_async_remote_copy(
            src_ref=integrals_ref.at[pl.ds(c * step, step), :, quarter(s, rep)],
            dst_ref=ints.at[slot, pl.ds(c * step, step)],
            send_sem=ints_send.at[s, c],
            recv_sem=ints_recv.at[slot, c],
            device_id=device(me, s, rep),
            device_id_type=MESH,
        )

    for c in range(chunks):
        for s in sub_peers:
            ints_copy(s, c, sub).start()

    def cnt_copy(pair, slot):
        return pltpu.make_async_remote_copy(
            src_ref=counts_ref,
            dst_ref=counts_all.at[slot],
            send_sem=cnt_send.at[pair],
            recv_sem=cnt_recv.at[slot],
            device_id=device(pair, sub, rep),
            device_id_type=MESH,
        )

    for pair in pair_peers:
        cnt_copy(pair, me).start()
    counts_all[me] = counts_ref[...]

    den_copy.wait()

    def den_send_copy(pair, h, slot_pair, slot_rep):
        return pltpu.make_async_remote_copy(
            src_ref=pack.at[pair, h],
            dst_ref=arrived.at[slot_rep, pl.ds(slot_pair * cap, cap)],
            send_sem=den_send.at[pair, h],
            recv_sem=den_recv.at[slot_pair, slot_rep],
            device_id=device(pair, sub, h),
            device_id_type=MESH,
        )

    unroll = divisor(cap, (8, 6, 4, 3, 2))

    def pack_for(pair):
        def body(i, carry):
            for u in range(unroll):
                r = i * unroll + u
                k = src_ref[pair * cap + r]
                row = den[k]
                for h in range(nrep):
                    pack[pair, h, r] = row[:, h * xq : (h + 1) * xq]
            return carry

        lax.fori_loop(0, cap // unroll, body, 0)

    for pair in pair_order:
        pack_for(pair)
        for h in [rep] + rep_peers:
            den_send_copy(pair, h, me, rep).start()
    pack_for(me)
    for h in rep_peers:
        den_send_copy(me, h, me, rep).start()
    own_den = pltpu.make_async_copy(
        pack.at[me, rep], arrived.at[rep, pl.ds(me * cap, cap)], local_sem
    )
    own_den.start()

    for pair in pair_peers:
        cnt_copy(pair, pair).wait_recv()
    to_smem = pltpu.make_async_copy(counts_all, counts_smem, den_send.at[me, rep])
    to_smem.start()
    to_smem.wait()
    starts = []
    finish = []
    total = jnp.int32(0)
    for s in range(npairs):
        starts.append(total)
        starts_smem[s] = total
        total = total + counts_smem[s, 0, me]
        finish.append(total)

    def place(j, carry):
        anchor = jnp.int32(0)
        start = jnp.int32(0)
        for s in range(npairs - 1):
            past = j >= finish[s]
            anchor = anchor + jnp.where(past, 1, 0)
            start = jnp.where(past, finish[s], start)
        places_smem[j] = jnp.minimum(anchor * cap + j - start, npairs * cap - 1)
        return carry

    lax.fori_loop(0, blocks, place, 0)

    own_den.wait()
    own_copy.wait()
    for h in rep_peers:
        den_send_copy(me, rep, me, h).wait_recv()
    for pair in reversed(pair_order):
        for h in [rep] + rep_peers:
            den_send_copy(pair, rep, pair, h).wait_recv()

    def block_ints(j):
        return jnp.concatenate([ints[s, j] for s in range(nsub)], axis=0)

    fit_unroll = divisor(step, (12, 8, 6, 4, 3, 2))
    fit = jnp.zeros(fit_pairs.shape[1:], jnp.float32)
    for c in range(chunks):
        for s in sub_peers:
            ints_copy(s, c, s).wait_recv()

        def fit_body(i, acc):
            for u in range(fit_unroll):
                j = c * step + i * fit_unroll + u
                at = places_smem[j]
                rows = jnp.concatenate([arrived[h, at] for h in range(nrep)], axis=0)
                acc = acc + lax.dot_general(
                    rows,
                    block_ints(j),
                    (((1,), (1,)), ((), ())),
                    preferred_element_type=jnp.float32,
                )
            return acc

        fit = lax.fori_loop(0, step // fit_unroll, fit_body, fit)

    plane_me = sub * nrep + rep
    fit_plane[plane_me] = fit

    def plane_copy(s, r, slot):
        return pltpu.make_async_remote_copy(
            src_ref=fit_plane.at[plane_me],
            dst_ref=fit_plane.at[slot],
            send_sem=plane_send.at[s * nrep + r],
            recv_sem=plane_recv.at[slot],
            device_id=device(me, s, r),
            device_id_type=MESH,
        )

    for s, r in plane_peers:
        plane_copy(s, r, plane_me).start()
    for s, r in plane_peers:
        plane_copy(s, r, s * nrep + r).wait_recv()
    fit = fit_plane[0]
    for i in range(1, nsub * nrep):
        fit = fit + fit_plane[i]
    fit_pairs[me] = fit

    def pairs_copy(pair, slot):
        return pltpu.make_async_remote_copy(
            src_ref=fit_pairs.at[me],
            dst_ref=fit_pairs.at[slot],
            send_sem=pairs_send.at[pair],
            recv_sem=pairs_recv.at[slot],
            device_id=device(pair, sub, rep),
            device_id_type=MESH,
        )

    for pair in pair_peers:
        pairs_copy(pair, me).start()
    for pair in pair_peers:
        pairs_copy(pair, pair).wait_recv()
    fit = fit_pairs[0]
    for i in range(1, npairs):
        fit = fit + fit_pairs[i]
    fitted = fit.astype(jnp.bfloat16)

    def ret_copy(pair, h, slot_pair, slot_rep):
        return pltpu.make_async_remote_copy(
            src_ref=ret.at[pair, h],
            dst_ref=homeward.at[slot_rep, pl.ds(slot_pair * cap, cap)],
            send_sem=ret_send.at[pair, h],
            recv_sem=ret_recv.at[slot_pair, slot_rep],
            device_id=device(pair, sub, h),
            device_id_type=MESH,
        )

    def coulomb_for(pair):
        start = starts_smem[pair]

        def body(i, carry):
            for u in range(unroll):
                r = i * unroll + u
                j = jnp.minimum(start + r, blocks - 1)
                rows = jnp.dot(
                    fitted, block_ints(j), preferred_element_type=jnp.float32
                ).astype(jnp.bfloat16)
                for h in range(nrep):
                    ret[pair, h, r] = rows[h * dens : (h + 1) * dens]
            return carry

        lax.fori_loop(0, cap // unroll, body, 0)

    for pair in pair_order:
        coulomb_for(pair)
        for h in [rep] + rep_peers:
            ret_copy(pair, h, me, rep).start()
    coulomb_for(me)
    for h in rep_peers:
        ret_copy(me, h, me, rep).start()
    own_ret = pltpu.make_async_copy(
        ret.at[me, rep], homeward.at[rep, pl.ds(me * cap, cap)], local_sem
    )
    own_ret.start()

    for c in range(chunks):
        for s in sub_peers:
            ints_copy(s, c, sub).wait_send()
    for pair in pair_peers:
        cnt_copy(pair, me).wait_send()
        pairs_copy(pair, me).wait_send()
    for s, r in plane_peers:
        plane_copy(s, r, plane_me).wait_send()
    for pair in pair_peers:
        for h in [rep] + rep_peers:
            den_send_copy(pair, h, me, rep).wait_send()
    for h in rep_peers:
        den_send_copy(me, h, me, rep).wait_send()

    own_ret.wait()
    for h in rep_peers:
        ret_copy(me, rep, me, h).wait_recv()
    for pair in reversed(pair_order):
        for h in [rep] + rep_peers:
            ret_copy(pair, rep, pair, h).wait_recv()

    out_unroll = divisor(blocks, (8, 6, 4, 3, 2))

    def out_body(i, carry):
        for u in range(out_unroll):
            k = i * out_unroll + u
            at = out_ids_ref[k]
            out_ref[k] = jnp.concatenate([homeward[h, at] for h in range(nrep)], axis=1)
        return carry

    lax.fori_loop(0, blocks // out_unroll, out_body, 0)

    for pair in pair_peers:
        for h in [rep] + rep_peers:
            ret_copy(pair, h, me, rep).wait_send()
    for h in rep_peers:
        ret_copy(me, h, me, rep).wait_send()


def on_device(integrals, density, block_owner):
    npairs = lax.axis_size("pairs")
    nsub = lax.axis_size("sub")
    nrep = lax.axis_size("rep")
    blocks, dens, width = density.shape
    p_dev = integrals.shape[1]
    xq = width // (nsub * nrep)
    cap = 2 * blocks // npairs
    chunks = divisor(blocks, (4, 3, 2))
    peer_ids = jnp.arange(npairs, dtype=jnp.int32)
    onehot = (block_owner[:, None] == peer_ids[None, :]).astype(jnp.int32)
    before = jnp.cumsum(onehot, axis=0) - onehot
    rank_in = jnp.sum(before * onehot, axis=1)
    outgoing = block_owner * cap + rank_in
    buffer_ids = jnp.arange(npairs * cap, dtype=jnp.int32)
    matches = (outgoing[None, :] == buffer_ids[:, None]).astype(jnp.int32)
    source_ids = jnp.sum(matches * jnp.arange(blocks, dtype=jnp.int32)[None, :], axis=1)
    lanes = jnp.arange(128, dtype=jnp.int32)
    counts = jnp.sum((block_owner[:, None] == lanes[None, :]).astype(jnp.int32), axis=0)
    counts = jnp.broadcast_to(counts[None, :], (8, 128))

    vmem = pl.BlockSpec(memory_space=pltpu.VMEM)
    smem = pl.BlockSpec(memory_space=pltpu.SMEM)
    anywhere = pl.BlockSpec(memory_space=pl.ANY)
    bf16 = jnp.bfloat16
    sems = pltpu.SemaphoreType.DMA
    rows = pl.pallas_call(
        functools.partial(exchange, npairs, nsub, nrep, chunks),
        out_shape=jax.ShapeDtypeStruct((blocks, dens, nrep * xq), bf16),
        in_specs=[smem, smem, vmem, anywhere, anywhere],
        out_specs=vmem,
        scratch_shapes=[
            pltpu.VMEM((nsub, blocks, p_dev, xq), bf16),
            pltpu.VMEM((blocks, dens, nrep * xq), bf16),
            pltpu.VMEM((npairs, nrep, cap, dens, xq), bf16),
            pltpu.VMEM((nrep, npairs * cap, dens, xq), bf16),
            pltpu.VMEM((npairs, nrep, cap, dens, xq), bf16),
            pltpu.VMEM((nrep, npairs * cap, dens, xq), bf16),
            pltpu.VMEM((npairs, 8, 128), jnp.int32),
            pltpu.SMEM((npairs, 8, 128), jnp.int32),
            pltpu.SMEM((npairs,), jnp.int32),
            pltpu.SMEM((blocks,), jnp.int32),
            pltpu.VMEM((nsub * nrep, nrep * dens, nsub * p_dev), jnp.float32),
            pltpu.VMEM((npairs, nrep * dens, nsub * p_dev), jnp.float32),
            sems,
            sems,
            sems((nsub, chunks)),
            sems((nsub, chunks)),
            sems((npairs, nrep)),
            sems((npairs, nrep)),
            sems((npairs, nrep)),
            sems((npairs, nrep)),
            sems((npairs,)),
            sems((npairs,)),
            sems((nsub * nrep,)),
            sems((nsub * nrep,)),
            sems((npairs,)),
            sems((npairs,)),
        ],
        compiler_params=pltpu.CompilerParams(
            collective_id=0, has_side_effects=True, vmem_limit_bytes=40 * 1024 * 1024
        ),
    )(source_ids, outgoing, counts, integrals, density)
    return rows.astype(jnp.float32)


def solution(mesh):
    in_specs = (
        P(("groups", "pairs"), "sub", None),
        P(("groups", "pairs"), "rep", None),
        P(("groups", "pairs")),
    )
    out_specs = P(("groups", "pairs"), "rep", "sub")
    return jax.shard_map(
        on_device, mesh=mesh, in_specs=in_specs, out_specs=out_specs, check_vma=False
    )
```

```python
import functools

import jax
import jax.numpy as jnp
from jax import lax
from jax.experimental import pallas as pl
from jax.experimental.pallas import tpu as pltpu
from jax.sharding import PartitionSpec as P

MESH = pl.DeviceIdType.MESH


def divisor(total, choices):
    for c in choices:
        if total % c == 0:
            return c
    return 1


def exchange(
    npairs,
    nsub,
    nrep,
    chunks,
    owner_ref,
    integrals_ref,
    density_ref,
    out_ref,
    ints,
    den,
    pack,
    arrived,
    ret,
    homeward,
    out_ids_ref,
    next_smem,
    counts_all,
    counts_smem,
    starts_smem,
    places_smem,
    fit_plane,
    fit_pairs,
    local_sem,
    own_sem,
    ints_send,
    ints_recv,
    den_send,
    den_recv,
    ret_send,
    ret_recv,
    cnt_send,
    cnt_recv,
    plane_send,
    plane_recv,
    pairs_send,
    pairs_recv,
):
    me = lax.axis_index("pairs")
    sub = lax.axis_index("sub")
    rep = lax.axis_index("rep")
    blocks, dens, _ = density_ref.shape
    xq = ints.shape[3]
    cap = arrived.shape[1] // npairs
    step = blocks // chunks

    def device(pair, s, r):
        return {"pairs": pair, "sub": s, "rep": r}

    def quarter(s, r):
        return pl.ds(pl.multiple_of((s * nrep + r) * xq, 128), xq)

    den_copy = pltpu.make_async_copy(
        density_ref.at[:, :, pl.ds(pl.multiple_of(sub * (nrep * xq), 128), nrep * xq)],
        den,
        local_sem,
    )
    den_copy.start()
    own_copy = pltpu.make_async_copy(
        integrals_ref.at[:, :, quarter(sub, rep)], ints.at[sub], own_sem
    )
    own_copy.start()

    pair_order = [lax.rem(me + npairs // 2 + i, npairs) for i in range(npairs - npairs // 2)] + [
        lax.rem(me + i, npairs) for i in range(1, npairs // 2)
    ]
    pair_peers = pair_order
    sub_peers = [lax.rem(sub + i, nsub) for i in range(1, nsub)]
    rep_peers = [lax.rem(rep + i, nrep) for i in range(1, nrep)]
    plane_peers = (
        [(sub, r) for r in rep_peers]
        + [(s, rep) for s in sub_peers]
        + [(s, r) for s in sub_peers for r in rep_peers]
    )

    barrier = pltpu.get_barrier_semaphore()
    greeted = 0
    for pair in pair_peers:
        for r in [rep] + rep_peers:
            pl.semaphore_signal(
                barrier, inc=1, device_id=device(pair, sub, r), device_id_type=MESH
            )
            greeted += 1
    for s, r in plane_peers:
        pl.semaphore_signal(barrier, inc=1, device_id=device(me, s, r), device_id_type=MESH)
        greeted += 1

    peer_range = range(npairs)

    def rank_body(k, seen):
        owner = owner_ref[k]
        at = owner * cap
        after = []
        for o in peer_range:
            mine = owner == o
            at = at + jnp.where(mine, seen[o], 0)
            after.append(seen[o] + jnp.where(mine, 1, 0))
        out_ids_ref[k] = at
        return tuple(after)

    sent = lax.fori_loop(0, blocks, rank_body, (jnp.int32(0),) * npairs)

    for o in peer_range:
        next_smem[o, blocks] = jnp.int32(blocks)

    def next_body(i, following):
        k = blocks - 1 - i
        owner = owner_ref[k]
        found = []
        for o in peer_range:
            found.append(jnp.where(owner == o, k, following[o]))
            next_smem[o, k] = found[o]
        return tuple(found)

    lax.fori_loop(0, blocks, next_body, (jnp.int32(blocks),) * npairs)

    lanes = lax.broadcasted_iota(jnp.int32, counts_all.shape[1:], 1)
    sent_row = jnp.zeros(counts_all.shape[1:], jnp.int32)
    for o in peer_range:
        sent_row = jnp.where(lanes == o, sent[o], sent_row)
    counts_all[me] = sent_row

    unroll = divisor(cap, (8, 6, 4, 3, 2))

    def pack_for(pair):
        def body(i, k):
            for u in range(unroll):
                r = i * unroll + u
                row = den[jnp.minimum(k, blocks - 1)]
                for h in range(nrep):
                    pack[pair, h, r] = row[:, h * xq : (h + 1) * xq]
                k = next_smem[pair, jnp.minimum(k + 1, blocks)]
            return k

        lax.fori_loop(0, cap // unroll, body, next_smem[pair, 0])

    den_copy.wait()
    for pair in pair_order:
        pack_for(pair)
    pl.semaphore_wait(barrier, greeted)

    def ints_copy(s, c, slot):
        return pltpu.make_async_remote_copy(
            src_ref=integrals_ref.at[pl.ds(c * step, step), :, quarter(s, rep)],
            dst_ref=ints.at[slot, pl.ds(c * step, step)],
            send_sem=ints_send.at[s, c],
            recv_sem=ints_recv.at[slot, c],
            device_id=device(me, s, rep),
            device_id_type=MESH,
        )

    def cnt_copy(pair, slot):
        return pltpu.make_async_remote_copy(
            src_ref=counts_all.at[me],
            dst_ref=counts_all.at[slot],
            send_sem=cnt_send.at[pair],
            recv_sem=cnt_recv.at[slot],
            device_id=device(pair, sub, rep),
            device_id_type=MESH,
        )

    def den_send_copy(pair, h, slot_pair, slot_rep):
        return pltpu.make_async_remote_copy(
            src_ref=pack.at[pair, h],
            dst_ref=arrived.at[slot_rep, pl.ds(slot_pair * cap, cap)],
            send_sem=den_send.at[pair, h],
            recv_sem=den_recv.at[slot_pair, slot_rep],
            device_id=device(pair, sub, h),
            device_id_type=MESH,
        )

    for pair in pair_peers:
        cnt_copy(pair, me).start()
    for pair in pair_order:
        for h in [rep] + rep_peers:
            den_send_copy(pair, h, me, rep).start()
    for c in range(chunks):
        for s in sub_peers:
            ints_copy(s, c, sub).start()
    pack_for(me)
    for h in rep_peers:
        den_send_copy(me, h, me, rep).start()
    own_den = pltpu.make_async_copy(
        pack.at[me, rep], arrived.at[rep, pl.ds(me * cap, cap)], local_sem
    )
    own_den.start()

    for pair in pair_peers:
        cnt_copy(pair, pair).wait_recv()
    to_smem = pltpu.make_async_copy(counts_all, counts_smem, den_send.at[me, rep])
    to_smem.start()
    to_smem.wait()
    starts = []
    finish = []
    total = jnp.int32(0)
    for s in range(npairs):
        starts.append(total)
        starts_smem[s] = total
        total = total + counts_smem[s, 0, me]
        finish.append(total)

    def place(j, carry):
        anchor = jnp.int32(0)
        start = jnp.int32(0)
        for s in range(npairs - 1):
            past = j >= finish[s]
            anchor = anchor + jnp.where(past, 1, 0)
            start = jnp.where(past, finish[s], start)
        places_smem[j] = jnp.minimum(anchor * cap + j - start, npairs * cap - 1)
        return carry

    lax.fori_loop(0, blocks, place, 0)

    own_den.wait()
    own_copy.wait()
    for h in rep_peers:
        den_send_copy(me, rep, me, h).wait_recv()
    for pair in reversed(pair_order):
        for h in [rep] + rep_peers:
            den_send_copy(pair, rep, pair, h).wait_recv()

    def block_ints(j):
        return jnp.concatenate([ints[s, j] for s in range(nsub)], axis=0)

    fit_unroll = divisor(step, (12, 8, 6, 4, 3, 2))
    fit = jnp.zeros(fit_pairs.shape[1:], jnp.float32)
    for c in range(chunks):
        for s in sub_peers:
            ints_copy(s, c, s).wait_recv()

        def fit_body(i, acc):
            for u in range(fit_unroll):
                j = c * step + i * fit_unroll + u
                at = places_smem[j]
                rows = jnp.concatenate([arrived[h, at] for h in range(nrep)], axis=0)
                acc = acc + lax.dot_general(
                    rows,
                    block_ints(j),
                    (((1,), (1,)), ((), ())),
                    preferred_element_type=jnp.float32,
                )
            return acc

        fit = lax.fori_loop(0, step // fit_unroll, fit_body, fit)

    plane_me = sub * nrep + rep
    fit_plane[plane_me] = fit

    def plane_copy(s, r, slot):
        return pltpu.make_async_remote_copy(
            src_ref=fit_plane.at[plane_me],
            dst_ref=fit_plane.at[slot],
            send_sem=plane_send.at[s * nrep + r],
            recv_sem=plane_recv.at[slot],
            device_id=device(me, s, r),
            device_id_type=MESH,
        )

    for s, r in plane_peers:
        plane_copy(s, r, plane_me).start()
    for s, r in plane_peers:
        plane_copy(s, r, s * nrep + r).wait_recv()
    fit = fit_plane[0]
    for i in range(1, nsub * nrep):
        fit = fit + fit_plane[i]
    fit_pairs[me] = fit

    def pairs_copy(pair, slot):
        return pltpu.make_async_remote_copy(
            src_ref=fit_pairs.at[me],
            dst_ref=fit_pairs.at[slot],
            send_sem=pairs_send.at[pair],
            recv_sem=pairs_recv.at[slot],
            device_id=device(pair, sub, rep),
            device_id_type=MESH,
        )

    for pair in pair_peers:
        pairs_copy(pair, me).start()
    for pair in pair_peers:
        pairs_copy(pair, pair).wait_recv()
    fit = fit_pairs[0]
    for i in range(1, npairs):
        fit = fit + fit_pairs[i]
    fitted = fit.astype(jnp.bfloat16)

    def ret_copy(pair, h, slot_pair, slot_rep):
        return pltpu.make_async_remote_copy(
            src_ref=ret.at[pair, h],
            dst_ref=homeward.at[slot_rep, pl.ds(slot_pair * cap, cap)],
            send_sem=ret_send.at[pair, h],
            recv_sem=ret_recv.at[slot_pair, slot_rep],
            device_id=device(pair, sub, h),
            device_id_type=MESH,
        )

    def coulomb_for(pair):
        start = starts_smem[pair]

        def body(i, carry):
            for u in range(unroll):
                r = i * unroll + u
                j = jnp.minimum(start + r, blocks - 1)
                rows = jnp.dot(
                    fitted, block_ints(j), preferred_element_type=jnp.float32
                ).astype(jnp.bfloat16)
                for h in range(nrep):
                    ret[pair, h, r] = rows[h * dens : (h + 1) * dens]
            return carry

        lax.fori_loop(0, cap // unroll, body, 0)

    for pair in pair_order:
        coulomb_for(pair)
        for h in [rep] + rep_peers:
            ret_copy(pair, h, me, rep).start()
    coulomb_for(me)
    for h in rep_peers:
        ret_copy(me, h, me, rep).start()
    own_ret = pltpu.make_async_copy(
        ret.at[me, rep], homeward.at[rep, pl.ds(me * cap, cap)], local_sem
    )
    own_ret.start()

    for c in range(chunks):
        for s in sub_peers:
            ints_copy(s, c, sub).wait_send()
    for pair in pair_peers:
        cnt_copy(pair, me).wait_send()
        pairs_copy(pair, me).wait_send()
    for s, r in plane_peers:
        plane_copy(s, r, plane_me).wait_send()
    for pair in pair_peers:
        for h in [rep] + rep_peers:
            den_send_copy(pair, h, me, rep).wait_send()
    for h in rep_peers:
        den_send_copy(me, h, me, rep).wait_send()

    own_ret.wait()
    for h in rep_peers:
        ret_copy(me, rep, me, h).wait_recv()
    for pair in reversed(pair_order):
        for h in [rep] + rep_peers:
            ret_copy(pair, rep, pair, h).wait_recv()

    out_unroll = divisor(blocks, (8, 6, 4, 3, 2))

    def out_body(i, carry):
        for u in range(out_unroll):
            k = i * out_unroll + u
            at = out_ids_ref[k]
            out_ref[k] = jnp.concatenate([homeward[h, at] for h in range(nrep)], axis=1)
        return carry

    lax.fori_loop(0, blocks // out_unroll, out_body, 0)

    for pair in pair_peers:
        for h in [rep] + rep_peers:
            ret_copy(pair, h, me, rep).wait_send()
    for h in rep_peers:
        ret_copy(me, h, me, rep).wait_send()


def on_device(integrals, density, block_owner):
    npairs = lax.axis_size("pairs")
    nsub = lax.axis_size("sub")
    nrep = lax.axis_size("rep")
    blocks, dens, width = density.shape
    p_dev = integrals.shape[1]
    xq = width // (nsub * nrep)
    cap = 2 * blocks // npairs
    chunks = divisor(blocks, (4, 3, 2))
    vmem = pl.BlockSpec(memory_space=pltpu.VMEM)
    smem = pl.BlockSpec(memory_space=pltpu.SMEM)
    hbm = pl.BlockSpec(memory_space=pltpu.HBM)
    bf16 = jnp.bfloat16
    sems = pltpu.SemaphoreType.DMA
    rows = pl.pallas_call(
        functools.partial(exchange, npairs, nsub, nrep, chunks),
        out_shape=jax.ShapeDtypeStruct((blocks, dens, nrep * xq), bf16),
        in_specs=[smem, hbm, hbm],
        out_specs=vmem,
        scratch_shapes=[
            pltpu.VMEM((nsub, blocks, p_dev, xq), bf16),
            pltpu.VMEM((blocks, dens, nrep * xq), bf16),
            pltpu.VMEM((npairs, nrep, cap, dens, xq), bf16),
            pltpu.VMEM((nrep, npairs * cap, dens, xq), bf16),
            pltpu.VMEM((npairs, nrep, cap, dens, xq), bf16),
            pltpu.VMEM((nrep, npairs * cap, dens, xq), bf16),
            pltpu.SMEM((blocks,), jnp.int32),
            pltpu.SMEM((npairs, blocks + 1), jnp.int32),
            pltpu.VMEM((npairs, 8, 128), jnp.int32),
            pltpu.SMEM((npairs, 8, 128), jnp.int32),
            pltpu.SMEM((npairs,), jnp.int32),
            pltpu.SMEM((blocks,), jnp.int32),
            pltpu.VMEM((nsub * nrep, nrep * dens, nsub * p_dev), jnp.float32),
            pltpu.VMEM((npairs, nrep * dens, nsub * p_dev), jnp.float32),
            sems,
            sems,
            sems((nsub, chunks)),
            sems((nsub, chunks)),
            sems((npairs, nrep)),
            sems((npairs, nrep)),
            sems((npairs, nrep)),
            sems((npairs, nrep)),
            sems((npairs,)),
            sems((npairs,)),
            sems((nsub * nrep,)),
            sems((nsub * nrep,)),
            sems((npairs,)),
            sems((npairs,)),
        ],
        compiler_params=pltpu.CompilerParams(
            collective_id=0, has_side_effects=True, vmem_limit_bytes=56 * 1024 * 1024
        ),
    )(block_owner, integrals, density)
    return rows.astype(jnp.float32)


def solution(mesh):
    in_specs = (
        P(("groups", "pairs"), "sub", None),
        P(("groups", "pairs"), "rep", None),
        P(("groups", "pairs")),
    )
    out_specs = P(("groups", "pairs"), "rep", "sub")
    return jax.shard_map(
        on_device, mesh=mesh, in_specs=in_specs, out_specs=out_specs, check_vma=False
    )
```

```python
import functools

import jax
import jax.numpy as jnp
from jax import lax
from jax.experimental import pallas as pl
from jax.experimental.pallas import tpu as pltpu
from jax.sharding import PartitionSpec as P

MESH = pl.DeviceIdType.MESH


def divisor(total, choices):
    for c in choices:
        if total % c == 0:
            return c
    return 1


def exchange(
    npairs,
    nsub,
    nrep,
    chunks,
    owner_ref,
    integrals_ref,
    density_ref,
    out_ref,
    ints,
    den,
    pack,
    arrived,
    ret,
    homeward,
    out_ids_ref,
    next_smem,
    counts_all,
    counts_smem,
    starts_smem,
    places_smem,
    fit_plane,
    fit_pairs,
    local_sem,
    own_sem,
    ints_send,
    ints_recv,
    den_send,
    den_recv,
    ret_send,
    ret_recv,
    cnt_send,
    cnt_recv,
    plane_send,
    plane_recv,
    pairs_send,
    pairs_recv,
):
    me = lax.axis_index("pairs")
    sub = lax.axis_index("sub")
    rep = lax.axis_index("rep")
    blocks, dens, _ = density_ref.shape
    xq = ints.shape[3]
    cap = arrived.shape[1] // npairs
    step = blocks // chunks

    def device(pair, s, r):
        return {"pairs": pair, "sub": s, "rep": r}

    def quarter(s, r):
        return pl.ds(pl.multiple_of((s * nrep + r) * xq, 128), xq)

    den_copy = pltpu.make_async_copy(
        density_ref.at[:, :, pl.ds(pl.multiple_of(sub * (nrep * xq), 128), nrep * xq)],
        den,
        local_sem,
    )
    den_copy.start()
    own_copy = pltpu.make_async_copy(
        integrals_ref.at[:, :, quarter(sub, rep)], ints.at[sub], own_sem
    )
    own_copy.start()

    pair_order = [lax.rem(me + npairs // 2 + i, npairs) for i in range(npairs - npairs // 2)] + [
        lax.rem(me + i, npairs) for i in range(1, npairs // 2)
    ]
    pair_peers = pair_order
    sub_peers = [lax.rem(sub + i, nsub) for i in range(1, nsub)]
    rep_peers = [lax.rem(rep + i, nrep) for i in range(1, nrep)]
    plane_peers = (
        [(sub, r) for r in rep_peers]
        + [(s, rep) for s in sub_peers]
        + [(s, r) for s in sub_peers for r in rep_peers]
    )

    barrier = pltpu.get_barrier_semaphore()
    greeted = 0
    for pair in pair_peers:
        for r in [rep] + rep_peers:
            pl.semaphore_signal(
                barrier, inc=1, device_id=device(pair, sub, r), device_id_type=MESH
            )
            greeted += 1
    for s, r in plane_peers:
        pl.semaphore_signal(barrier, inc=1, device_id=device(me, s, r), device_id_type=MESH)
        greeted += 1

    peer_range = range(npairs)

    def rank_body(k, seen):
        owner = owner_ref[k]
        at = owner * cap
        after = []
        for o in peer_range:
            mine = owner == o
            at = at + jnp.where(mine, seen[o], 0)
            after.append(seen[o] + jnp.where(mine, 1, 0))
        out_ids_ref[k] = at
        return tuple(after)

    sent = lax.fori_loop(0, blocks, rank_body, (jnp.int32(0),) * npairs)

    for o in peer_range:
        next_smem[o, blocks] = jnp.int32(blocks)

    def next_body(i, following):
        k = blocks - 1 - i
        owner = owner_ref[k]
        found = []
        for o in peer_range:
            found.append(jnp.where(owner == o, k, following[o]))
            next_smem[o, k] = found[o]
        return tuple(found)

    lax.fori_loop(0, blocks, next_body, (jnp.int32(blocks),) * npairs)

    lanes = lax.broadcasted_iota(jnp.int32, counts_all.shape[1:], 1)
    sent_row = jnp.zeros(counts_all.shape[1:], jnp.int32)
    for o in peer_range:
        sent_row = jnp.where(lanes == o, sent[o], sent_row)
    counts_all[me] = sent_row

    unroll = divisor(cap, (8, 6, 4, 3, 2))

    def pack_for(pair):
        def body(i, k):
            for u in range(unroll):
                r = i * unroll + u
                row = den[jnp.minimum(k, blocks - 1)]
                for h in range(nrep):
                    pack[pair, h, r] = row[:, h * xq : (h + 1) * xq]
                k = next_smem[pair, jnp.minimum(k + 1, blocks)]
            return k

        lax.fori_loop(0, cap // unroll, body, next_smem[pair, 0])

    den_copy.wait()
    pack_for(pair_order[0])
    pl.semaphore_wait(barrier, greeted)

    def ints_copy(s, c, slot):
        return pltpu.make_async_remote_copy(
            src_ref=integrals_ref.at[pl.ds(c * step, step), :, quarter(s, rep)],
            dst_ref=ints.at[slot, pl.ds(c * step, step)],
            send_sem=ints_send.at[s, c],
            recv_sem=ints_recv.at[slot, c],
            device_id=device(me, s, rep),
            device_id_type=MESH,
        )

    def cnt_copy(pair, slot):
        return pltpu.make_async_remote_copy(
            src_ref=counts_all.at[me],
            dst_ref=counts_all.at[slot],
            send_sem=cnt_send.at[pair],
            recv_sem=cnt_recv.at[slot],
            device_id=device(pair, sub, rep),
            device_id_type=MESH,
        )

    def den_send_copy(pair, h, slot_pair, slot_rep):
        return pltpu.make_async_remote_copy(
            src_ref=pack.at[pair, h],
            dst_ref=arrived.at[slot_rep, pl.ds(slot_pair * cap, cap)],
            send_sem=den_send.at[pair, h],
            recv_sem=den_recv.at[slot_pair, slot_rep],
            device_id=device(pair, sub, h),
            device_id_type=MESH,
        )

    for pair in pair_peers:
        cnt_copy(pair, me).start()
    for i, pair in enumerate(pair_order):
        if i > 0:
            pack_for(pair)
        for h in [rep] + rep_peers:
            den_send_copy(pair, h, me, rep).start()
        if i == 0:
            for c in range(chunks):
                for s in sub_peers:
                    ints_copy(s, c, sub).start()
    pack_for(me)
    for h in rep_peers:
        den_send_copy(me, h, me, rep).start()
    own_den = pltpu.make_async_copy(
        pack.at[me, rep], arrived.at[rep, pl.ds(me * cap, cap)], local_sem
    )
    own_den.start()

    for pair in pair_peers:
        cnt_copy(pair, pair).wait_recv()
    to_smem = pltpu.make_async_copy(counts_all, counts_smem, den_send.at[me, rep])
    to_smem.start()
    to_smem.wait()
    starts = []
    finish = []
    total = jnp.int32(0)
    for s in range(npairs):
        starts.append(total)
        starts_smem[s] = total
        total = total + counts_smem[s, 0, me]
        finish.append(total)

    def place(j, carry):
        anchor = jnp.int32(0)
        start = jnp.int32(0)
        for s in range(npairs - 1):
            past = j >= finish[s]
            anchor = anchor + jnp.where(past, 1, 0)
            start = jnp.where(past, finish[s], start)
        places_smem[j] = jnp.minimum(anchor * cap + j - start, npairs * cap - 1)
        return carry

    lax.fori_loop(0, blocks, place, 0)

    own_den.wait()
    own_copy.wait()
    for h in rep_peers:
        den_send_copy(me, rep, me, h).wait_recv()
    for pair in reversed(pair_order):
        for h in [rep] + rep_peers:
            den_send_copy(pair, rep, pair, h).wait_recv()

    def block_ints(j):
        return jnp.concatenate([ints[s, j] for s in range(nsub)], axis=0)

    fit_unroll = divisor(step, (12, 8, 6, 4, 3, 2))
    fit = jnp.zeros(fit_pairs.shape[1:], jnp.float32)
    for c in range(chunks):
        for s in sub_peers:
            ints_copy(s, c, s).wait_recv()

        def fit_body(i, acc):
            for u in range(fit_unroll):
                j = c * step + i * fit_unroll + u
                at = places_smem[j]
                rows = jnp.concatenate([arrived[h, at] for h in range(nrep)], axis=0)
                acc = acc + lax.dot_general(
                    rows,
                    block_ints(j),
                    (((1,), (1,)), ((), ())),
                    preferred_element_type=jnp.float32,
                )
            return acc

        fit = lax.fori_loop(0, step // fit_unroll, fit_body, fit)

    plane_me = sub * nrep + rep
    fit_plane[plane_me] = fit

    def plane_copy(s, r, slot):
        return pltpu.make_async_remote_copy(
            src_ref=fit_plane.at[plane_me],
            dst_ref=fit_plane.at[slot],
            send_sem=plane_send.at[s * nrep + r],
            recv_sem=plane_recv.at[slot],
            device_id=device(me, s, r),
            device_id_type=MESH,
        )

    for s, r in plane_peers:
        plane_copy(s, r, plane_me).start()
    for s, r in plane_peers:
        plane_copy(s, r, s * nrep + r).wait_recv()
    fit = fit_plane[0]
    for i in range(1, nsub * nrep):
        fit = fit + fit_plane[i]
    fit_pairs[me] = fit

    def pairs_copy(pair, slot):
        return pltpu.make_async_remote_copy(
            src_ref=fit_pairs.at[me],
            dst_ref=fit_pairs.at[slot],
            send_sem=pairs_send.at[pair],
            recv_sem=pairs_recv.at[slot],
            device_id=device(pair, sub, rep),
            device_id_type=MESH,
        )

    for pair in pair_peers:
        pairs_copy(pair, me).start()
    for pair in pair_peers:
        pairs_copy(pair, pair).wait_recv()
    fit = fit_pairs[0]
    for i in range(1, npairs):
        fit = fit + fit_pairs[i]
    fitted = fit.astype(jnp.bfloat16)

    def ret_copy(pair, h, slot_pair, slot_rep):
        return pltpu.make_async_remote_copy(
            src_ref=ret.at[pair, h],
            dst_ref=homeward.at[slot_rep, pl.ds(slot_pair * cap, cap)],
            send_sem=ret_send.at[pair, h],
            recv_sem=ret_recv.at[slot_pair, slot_rep],
            device_id=device(pair, sub, h),
            device_id_type=MESH,
        )

    def coulomb_for(pair):
        start = starts_smem[pair]

        def body(i, carry):
            for u in range(unroll):
                r = i * unroll + u
                j = jnp.minimum(start + r, blocks - 1)
                rows = jnp.dot(
                    fitted, block_ints(j), preferred_element_type=jnp.float32
                ).astype(jnp.bfloat16)
                for h in range(nrep):
                    ret[pair, h, r] = rows[h * dens : (h + 1) * dens]
            return carry

        lax.fori_loop(0, cap // unroll, body, 0)

    for pair in pair_order:
        coulomb_for(pair)
        for h in [rep] + rep_peers:
            ret_copy(pair, h, me, rep).start()
    coulomb_for(me)
    for h in rep_peers:
        ret_copy(me, h, me, rep).start()
    own_ret = pltpu.make_async_copy(
        ret.at[me, rep], homeward.at[rep, pl.ds(me * cap, cap)], local_sem
    )
    own_ret.start()

    for c in range(chunks):
        for s in sub_peers:
            ints_copy(s, c, sub).wait_send()
    for pair in pair_peers:
        cnt_copy(pair, me).wait_send()
        pairs_copy(pair, me).wait_send()
    for s, r in plane_peers:
        plane_copy(s, r, plane_me).wait_send()
    for pair in pair_peers:
        for h in [rep] + rep_peers:
            den_send_copy(pair, h, me, rep).wait_send()
    for h in rep_peers:
        den_send_copy(me, h, me, rep).wait_send()

    own_ret.wait()
    for h in rep_peers:
        ret_copy(me, rep, me, h).wait_recv()
    for pair in reversed(pair_order):
        for h in [rep] + rep_peers:
            ret_copy(pair, rep, pair, h).wait_recv()

    out_unroll = divisor(blocks, (8, 6, 4, 3, 2))

    def out_body(i, carry):
        for u in range(out_unroll):
            k = i * out_unroll + u
            at = out_ids_ref[k]
            out_ref[k] = jnp.concatenate([homeward[h, at] for h in range(nrep)], axis=1)
        return carry

    lax.fori_loop(0, blocks // out_unroll, out_body, 0)

    for pair in pair_peers:
        for h in [rep] + rep_peers:
            ret_copy(pair, h, me, rep).wait_send()
    for h in rep_peers:
        ret_copy(me, h, me, rep).wait_send()


def on_device(integrals, density, block_owner):
    npairs = lax.axis_size("pairs")
    nsub = lax.axis_size("sub")
    nrep = lax.axis_size("rep")
    blocks, dens, width = density.shape
    p_dev = integrals.shape[1]
    xq = width // (nsub * nrep)
    cap = 2 * blocks // npairs
    chunks = divisor(blocks, (4, 3, 2))
    vmem = pl.BlockSpec(memory_space=pltpu.VMEM)
    smem = pl.BlockSpec(memory_space=pltpu.SMEM)
    hbm = pl.BlockSpec(memory_space=pltpu.HBM)
    bf16 = jnp.bfloat16
    sems = pltpu.SemaphoreType.DMA
    rows = pl.pallas_call(
        functools.partial(exchange, npairs, nsub, nrep, chunks),
        out_shape=jax.ShapeDtypeStruct((blocks, dens, nrep * xq), bf16),
        in_specs=[smem, hbm, hbm],
        out_specs=vmem,
        scratch_shapes=[
            pltpu.VMEM((nsub, blocks, p_dev, xq), bf16),
            pltpu.VMEM((blocks, dens, nrep * xq), bf16),
            pltpu.VMEM((npairs, nrep, cap, dens, xq), bf16),
            pltpu.VMEM((nrep, npairs * cap, dens, xq), bf16),
            pltpu.VMEM((npairs, nrep, cap, dens, xq), bf16),
            pltpu.VMEM((nrep, npairs * cap, dens, xq), bf16),
            pltpu.SMEM((blocks,), jnp.int32),
            pltpu.SMEM((npairs, blocks + 1), jnp.int32),
            pltpu.VMEM((npairs, 8, 128), jnp.int32),
            pltpu.SMEM((npairs, 8, 128), jnp.int32),
            pltpu.SMEM((npairs,), jnp.int32),
            pltpu.SMEM((blocks,), jnp.int32),
            pltpu.VMEM((nsub * nrep, nrep * dens, nsub * p_dev), jnp.float32),
            pltpu.VMEM((npairs, nrep * dens, nsub * p_dev), jnp.float32),
            sems,
            sems,
            sems((nsub, chunks)),
            sems((nsub, chunks)),
            sems((npairs, nrep)),
            sems((npairs, nrep)),
            sems((npairs, nrep)),
            sems((npairs, nrep)),
            sems((npairs,)),
            sems((npairs,)),
            sems((nsub * nrep,)),
            sems((nsub * nrep,)),
            sems((npairs,)),
            sems((npairs,)),
        ],
        compiler_params=pltpu.CompilerParams(
            collective_id=0, has_side_effects=True, vmem_limit_bytes=56 * 1024 * 1024
        ),
    )(block_owner, integrals, density)
    return rows.astype(jnp.float32)


def solution(mesh):
    in_specs = (
        P(("groups", "pairs"), "sub", None),
        P(("groups", "pairs"), "rep", None),
        P(("groups", "pairs")),
    )
    out_specs = P(("groups", "pairs"), "rep", "sub")
    return jax.shard_map(
        on_device, mesh=mesh, in_specs=in_specs, out_specs=out_specs, check_vma=False
    )
```

```python
import functools

import jax
import jax.numpy as jnp
from jax import lax
from jax.experimental import pallas as pl
from jax.experimental.pallas import tpu as pltpu
from jax.sharding import PartitionSpec as P

MESH = pl.DeviceIdType.MESH


def divisor(total, choices):
    for c in choices:
        if total % c == 0:
            return c
    return 1


def exchange(
    npairs,
    nsub,
    nrep,
    chunks,
    owner_ref,
    integrals_ref,
    density_ref,
    out_ref,
    ints,
    den,
    pack,
    arrived,
    ret,
    homeward,
    out_ids_ref,
    next_smem,
    counts_all,
    counts_smem,
    starts_smem,
    places_smem,
    fit_plane,
    fit_pairs,
    local_sem,
    own_sem,
    ints_send,
    ints_recv,
    den_send,
    den_recv,
    ret_send,
    ret_recv,
    cnt_send,
    cnt_recv,
    plane_send,
    plane_recv,
    pairs_send,
    pairs_recv,
):
    me = lax.axis_index("pairs")
    sub = lax.axis_index("sub")
    rep = lax.axis_index("rep")
    blocks, dens, _ = density_ref.shape
    xq = ints.shape[3]
    cap = arrived.shape[1] // npairs
    step = blocks // chunks

    def device(pair, s, r):
        return {"pairs": pair, "sub": s, "rep": r}

    def quarter(s, r):
        return pl.ds(pl.multiple_of((s * nrep + r) * xq, 128), xq)

    den_copy = pltpu.make_async_copy(
        density_ref.at[:, :, pl.ds(pl.multiple_of(sub * (nrep * xq), 128), nrep * xq)],
        den,
        local_sem,
    )
    den_copy.start()
    own_copy = pltpu.make_async_copy(
        integrals_ref.at[:, :, quarter(sub, rep)], ints.at[sub], own_sem
    )
    own_copy.start()

    pair_order = [lax.rem(me + npairs // 2 + i, npairs) for i in range(npairs - npairs // 2)] + [
        lax.rem(me + i, npairs) for i in range(1, npairs // 2)
    ]
    pair_peers = pair_order
    sub_peers = [lax.rem(sub + i, nsub) for i in range(1, nsub)]
    rep_peers = [lax.rem(rep + i, nrep) for i in range(1, nrep)]
    plane_peers = (
        [(sub, r) for r in rep_peers]
        + [(s, rep) for s in sub_peers]
        + [(s, r) for s in sub_peers for r in rep_peers]
    )

    barrier = pltpu.get_barrier_semaphore()
    greeted = 0
    for pair in pair_peers:
        for r in [rep] + rep_peers:
            pl.semaphore_signal(
                barrier, inc=1, device_id=device(pair, sub, r), device_id_type=MESH
            )
            greeted += 1
    for s, r in plane_peers:
        pl.semaphore_signal(barrier, inc=1, device_id=device(me, s, r), device_id_type=MESH)
        greeted += 1

    peer_range = range(npairs)

    def rank_body(k, seen):
        owner = owner_ref[k]
        at = owner * cap
        after = []
        for o in peer_range:
            mine = owner == o
            at = at + jnp.where(mine, seen[o], 0)
            after.append(seen[o] + jnp.where(mine, 1, 0))
        out_ids_ref[k] = at
        return tuple(after)

    sent = lax.fori_loop(0, blocks, rank_body, (jnp.int32(0),) * npairs)

    for o in peer_range:
        next_smem[o, blocks] = jnp.int32(blocks)

    def next_body(i, following):
        k = blocks - 1 - i
        owner = owner_ref[k]
        found = []
        for o in peer_range:
            found.append(jnp.where(owner == o, k, following[o]))
            next_smem[o, k] = found[o]
        return tuple(found)

    lax.fori_loop(0, blocks, next_body, (jnp.int32(blocks),) * npairs)

    lanes = lax.broadcasted_iota(jnp.int32, counts_all.shape[1:], 1)
    sent_row = jnp.zeros(counts_all.shape[1:], jnp.int32)
    for o in peer_range:
        sent_row = jnp.where(lanes == o, sent[o], sent_row)
    counts_all[me] = sent_row

    unroll = divisor(cap, (8, 6, 4, 3, 2))

    def pack_for(pair):
        def body(i, k):
            for u in range(unroll):
                r = i * unroll + u
                row = den[jnp.minimum(k, blocks - 1)]
                for h in range(nrep):
                    pack[pair, h, r] = row[:, h * xq : (h + 1) * xq]
                k = next_smem[pair, jnp.minimum(k + 1, blocks)]
            return k

        lax.fori_loop(0, cap // unroll, body, next_smem[pair, 0])

    den_copy.wait()
    pack_for(pair_order[0])
    pl.semaphore_wait(barrier, greeted)

    def ints_copy(s, c, slot):
        return pltpu.make_async_remote_copy(
            src_ref=integrals_ref.at[pl.ds(c * step, step), :, quarter(s, rep)],
            dst_ref=ints.at[slot, pl.ds(c * step, step)],
            send_sem=ints_send.at[s, c],
            recv_sem=ints_recv.at[slot, c],
            device_id=device(me, s, rep),
            device_id_type=MESH,
        )

    def cnt_copy(pair, slot):
        return pltpu.make_async_remote_copy(
            src_ref=counts_all.at[me],
            dst_ref=counts_all.at[slot],
            send_sem=cnt_send.at[pair],
            recv_sem=cnt_recv.at[slot],
            device_id=device(pair, sub, rep),
            device_id_type=MESH,
        )

    def den_send_copy(pair, h, slot_pair, slot_rep):
        return pltpu.make_async_remote_copy(
            src_ref=pack.at[pair, h],
            dst_ref=arrived.at[slot_rep, pl.ds(slot_pair * cap, cap)],
            send_sem=den_send.at[pair, h],
            recv_sem=den_recv.at[slot_pair, slot_rep],
            device_id=device(pair, sub, h),
            device_id_type=MESH,
        )

    for pair in pair_peers:
        cnt_copy(pair, me).start()
    for i, pair in enumerate(pair_order):
        if i > 0:
            pack_for(pair)
        for h in [rep] + rep_peers:
            den_send_copy(pair, h, me, rep).start()
        if i == 0:
            for c in range(chunks):
                for s in sub_peers:
                    ints_copy(s, c, sub).start()
    pack_for(me)
    for h in rep_peers:
        den_send_copy(me, h, me, rep).start()
    own_den = pltpu.make_async_copy(
        pack.at[me, rep], arrived.at[rep, pl.ds(me * cap, cap)], local_sem
    )
    own_den.start()

    for pair in pair_peers:
        cnt_copy(pair, pair).wait_recv()
    to_smem = pltpu.make_async_copy(counts_all, counts_smem, den_send.at[me, rep])
    to_smem.start()
    to_smem.wait()
    starts = []
    finish = []
    total = jnp.int32(0)
    for s in range(npairs):
        starts.append(total)
        starts_smem[s] = total
        total = total + counts_smem[s, 0, me]
        finish.append(total)

    def place(j, carry):
        anchor = jnp.int32(0)
        start = jnp.int32(0)
        for s in range(npairs - 1):
            past = j >= finish[s]
            anchor = anchor + jnp.where(past, 1, 0)
            start = jnp.where(past, finish[s], start)
        places_smem[j] = jnp.minimum(anchor * cap + j - start, npairs * cap - 1)
        return carry

    lax.fori_loop(0, blocks, place, 0)

    own_den.wait()
    own_copy.wait()
    for h in rep_peers:
        den_send_copy(me, rep, me, h).wait_recv()
    for pair in reversed(pair_order):
        for h in [rep] + rep_peers:
            den_send_copy(pair, rep, pair, h).wait_recv()

    def block_ints(j):
        return jnp.concatenate([ints[s, j] for s in range(nsub)], axis=0)

    fit_unroll = divisor(step, (12, 8, 6, 4, 3, 2))
    fit = jnp.zeros(fit_pairs.shape[1:], jnp.float32)
    for c in range(chunks):
        for s in sub_peers:
            ints_copy(s, c, s).wait_recv()

        def fit_body(i, acc):
            for u in range(fit_unroll):
                j = c * step + i * fit_unroll + u
                at = places_smem[j]
                rows = jnp.concatenate([arrived[h, at] for h in range(nrep)], axis=0)
                acc = acc + lax.dot_general(
                    rows,
                    block_ints(j),
                    (((1,), (1,)), ((), ())),
                    preferred_element_type=jnp.float32,
                )
            return acc

        fit = lax.fori_loop(0, step // fit_unroll, fit_body, fit)

    plane_me = sub * nrep + rep
    fit_plane[plane_me] = fit

    def plane_copy(s, r, slot):
        return pltpu.make_async_remote_copy(
            src_ref=fit_plane.at[plane_me],
            dst_ref=fit_plane.at[slot],
            send_sem=plane_send.at[s * nrep + r],
            recv_sem=plane_recv.at[slot],
            device_id=device(me, s, r),
            device_id_type=MESH,
        )

    for s, r in plane_peers:
        plane_copy(s, r, plane_me).start()
    for s, r in plane_peers:
        plane_copy(s, r, s * nrep + r).wait_recv()
    fit = fit_plane[0]
    for i in range(1, nsub * nrep):
        fit = fit + fit_plane[i]
    fit_pairs[me] = fit

    def pairs_copy(pair, slot):
        return pltpu.make_async_remote_copy(
            src_ref=fit_pairs.at[me],
            dst_ref=fit_pairs.at[slot],
            send_sem=pairs_send.at[pair],
            recv_sem=pairs_recv.at[slot],
            device_id=device(pair, sub, rep),
            device_id_type=MESH,
        )

    for pair in pair_peers:
        pairs_copy(pair, me).start()
    for pair in pair_peers:
        pairs_copy(pair, pair).wait_recv()
    fit = fit_pairs[0]
    for i in range(1, npairs):
        fit = fit + fit_pairs[i]
    fitted = fit.astype(jnp.bfloat16)

    def ret_copy(pair, h, slot_pair, slot_rep):
        return pltpu.make_async_remote_copy(
            src_ref=ret.at[pair, h],
            dst_ref=homeward.at[slot_rep, pl.ds(slot_pair * cap, cap)],
            send_sem=ret_send.at[pair, h],
            recv_sem=ret_recv.at[slot_pair, slot_rep],
            device_id=device(pair, sub, h),
            device_id_type=MESH,
        )

    def coulomb_for(pair):
        start = starts_smem[pair]

        def body(i, carry):
            for u in range(unroll):
                r = i * unroll + u
                j = jnp.minimum(start + r, blocks - 1)
                rows = jnp.dot(
                    fitted, block_ints(j), preferred_element_type=jnp.float32
                ).astype(jnp.bfloat16)
                for h in range(nrep):
                    ret[pair, h, r] = rows[h * dens : (h + 1) * dens]
            return carry

        lax.fori_loop(0, cap // unroll, body, 0)

    for pair in pair_order:
        coulomb_for(pair)
        for h in [rep] + rep_peers:
            ret_copy(pair, h, me, rep).start()
    coulomb_for(me)
    for h in rep_peers:
        ret_copy(me, h, me, rep).start()
    own_ret = pltpu.make_async_copy(
        ret.at[me, rep], homeward.at[rep, pl.ds(me * cap, cap)], local_sem
    )
    own_ret.start()

    for c in range(chunks):
        for s in sub_peers:
            ints_copy(s, c, sub).wait_send()
    for pair in pair_peers:
        cnt_copy(pair, me).wait_send()
        pairs_copy(pair, me).wait_send()
    for s, r in plane_peers:
        plane_copy(s, r, plane_me).wait_send()
    for pair in pair_peers:
        for h in [rep] + rep_peers:
            den_send_copy(pair, h, me, rep).wait_send()
    for h in rep_peers:
        den_send_copy(me, h, me, rep).wait_send()

    own_ret.wait()
    for h in rep_peers:
        ret_copy(me, rep, me, h).wait_recv()
    for pair in reversed(pair_order):
        for h in [rep] + rep_peers:
            ret_copy(pair, rep, pair, h).wait_recv()

    out_unroll = divisor(blocks, (8, 6, 4, 3, 2))

    def out_body(i, carry):
        for u in range(out_unroll):
            k = i * out_unroll + u
            at = out_ids_ref[k]
            out_ref[k] = jnp.concatenate([homeward[h, at] for h in range(nrep)], axis=1)
        return carry

    lax.fori_loop(0, blocks // out_unroll, out_body, 0)

    for pair in pair_peers:
        for h in [rep] + rep_peers:
            ret_copy(pair, h, me, rep).wait_send()
    for h in rep_peers:
        ret_copy(me, h, me, rep).wait_send()


def on_device(integrals, density, block_owner):
    npairs = lax.axis_size("pairs")
    nsub = lax.axis_size("sub")
    nrep = lax.axis_size("rep")
    blocks, dens, width = density.shape
    p_dev = integrals.shape[1]
    xq = width // (nsub * nrep)
    cap = 2 * blocks // npairs
    chunks = divisor(blocks, (4, 3, 2))
    vmem = pl.BlockSpec(memory_space=pltpu.VMEM)
    smem = pl.BlockSpec(memory_space=pltpu.SMEM)
    hbm = pl.BlockSpec(memory_space=pltpu.HBM)
    bf16 = jnp.bfloat16
    sems = pltpu.SemaphoreType.DMA
    rows = pl.pallas_call(
        functools.partial(exchange, npairs, nsub, nrep, chunks),
        out_shape=jax.ShapeDtypeStruct((blocks, dens, nrep * xq), bf16),
        in_specs=[smem, hbm, hbm],
        out_specs=vmem,
        scratch_shapes=[
            pltpu.VMEM((nsub, blocks, p_dev, xq), bf16),
            pltpu.VMEM((blocks, dens, nrep * xq), bf16),
            pltpu.VMEM((npairs, nrep, cap, dens, xq), bf16),
            pltpu.VMEM((nrep, npairs * cap, dens, xq), bf16),
            pltpu.VMEM((npairs, nrep, cap, dens, xq), bf16),
            pltpu.VMEM((nrep, npairs * cap, dens, xq), bf16),
            pltpu.SMEM((blocks,), jnp.int32),
            pltpu.SMEM((npairs, blocks + 1), jnp.int32),
            pltpu.VMEM((npairs, 8, 128), jnp.int32),
            pltpu.SMEM((npairs, 8, 128), jnp.int32),
            pltpu.SMEM((npairs,), jnp.int32),
            pltpu.SMEM((blocks,), jnp.int32),
            pltpu.VMEM((nsub * nrep, nrep * dens, nsub * p_dev), jnp.float32),
            pltpu.VMEM((npairs, nrep * dens, nsub * p_dev), jnp.float32),
            sems,
            sems,
            sems((nsub, chunks)),
            sems((nsub, chunks)),
            sems((npairs, nrep)),
            sems((npairs, nrep)),
            sems((npairs, nrep)),
            sems((npairs, nrep)),
            sems((npairs,)),
            sems((npairs,)),
            sems((nsub * nrep,)),
            sems((nsub * nrep,)),
            sems((npairs,)),
            sems((npairs,)),
        ],
        compiler_params=pltpu.CompilerParams(
            collective_id=0, has_side_effects=True, vmem_limit_bytes=105 * 512 * 1024
        ),
    )(block_owner, integrals, density)
    return rows.astype(jnp.float32)


def solution(mesh):
    in_specs = (
        P(("groups", "pairs"), "sub", None),
        P(("groups", "pairs"), "rep", None),
        P(("groups", "pairs")),
    )
    out_specs = P(("groups", "pairs"), "rep", "sub")
    return jax.shard_map(
        on_device, mesh=mesh, in_specs=in_specs, out_specs=out_specs, check_vma=False
    )
```

```python
import functools

import jax
import jax.numpy as jnp
from jax import lax
from jax.experimental import pallas as pl
from jax.experimental.pallas import tpu as pltpu
from jax.sharding import PartitionSpec as P

MESH = pl.DeviceIdType.MESH


def divisor(total, choices):
    for c in choices:
        if total % c == 0:
            return c
    return 1


def exchange(
    npairs,
    nsub,
    nrep,
    chunks,
    owner_ref,
    integrals_ref,
    density_ref,
    out_ref,
    ints,
    den,
    pack,
    arrived,
    ret,
    homeward,
    out_ids_ref,
    next_smem,
    counts_all,
    counts_smem,
    starts_smem,
    places_smem,
    fit_plane,
    fit_pairs,
    local_sem,
    own_sem,
    ints_send,
    ints_recv,
    den_send,
    den_recv,
    ret_send,
    ret_recv,
    cnt_send,
    cnt_recv,
    plane_send,
    plane_recv,
    pairs_send,
    pairs_recv,
):
    me = lax.axis_index("pairs")
    sub = lax.axis_index("sub")
    rep = lax.axis_index("rep")
    blocks, dens, _ = density_ref.shape
    xq = ints.shape[3]
    cap = arrived.shape[1] // npairs
    step = blocks // chunks

    def device(pair, s, r):
        return {"pairs": pair, "sub": s, "rep": r}

    def quarter(s, r):
        return pl.ds(pl.multiple_of((s * nrep + r) * xq, 128), xq)

    den_copy = pltpu.make_async_copy(
        density_ref.at[:, :, pl.ds(pl.multiple_of(sub * (nrep * xq), 128), nrep * xq)],
        den,
        local_sem,
    )
    den_copy.start()
    own_copy = pltpu.make_async_copy(
        integrals_ref.at[:, :, quarter(sub, rep)], ints.at[sub], own_sem
    )
    own_copy.start()

    pair_order = [lax.rem(me + npairs // 2 + i, npairs) for i in range(npairs - npairs // 2)] + [
        lax.rem(me + i, npairs) for i in range(1, npairs // 2)
    ]
    pair_peers = pair_order
    sub_peers = [lax.rem(sub + i, nsub) for i in range(1, nsub)]
    rep_peers = [lax.rem(rep + i, nrep) for i in range(1, nrep)]
    plane_peers = (
        [(sub, r) for r in rep_peers]
        + [(s, rep) for s in sub_peers]
        + [(s, r) for s in sub_peers for r in rep_peers]
    )

    barrier = pltpu.get_barrier_semaphore()
    greeted = 0
    for pair in pair_peers:
        for r in [rep] + rep_peers:
            pl.semaphore_signal(
                barrier, inc=1, device_id=device(pair, sub, r), device_id_type=MESH
            )
            greeted += 1
    for s, r in plane_peers:
        pl.semaphore_signal(barrier, inc=1, device_id=device(me, s, r), device_id_type=MESH)
        greeted += 1

    peer_range = range(npairs)

    def rank_body(k, seen):
        owner = owner_ref[k]
        at = owner * cap
        after = []
        for o in peer_range:
            mine = owner == o
            at = at + jnp.where(mine, seen[o], 0)
            after.append(seen[o] + jnp.where(mine, 1, 0))
        out_ids_ref[k] = at
        return tuple(after)

    sent = lax.fori_loop(0, blocks, rank_body, (jnp.int32(0),) * npairs)

    for o in peer_range:
        next_smem[o, blocks] = jnp.int32(blocks)

    def next_body(i, following):
        k = blocks - 1 - i
        owner = owner_ref[k]
        found = []
        for o in peer_range:
            found.append(jnp.where(owner == o, k, following[o]))
            next_smem[o, k] = found[o]
        return tuple(found)

    lax.fori_loop(0, blocks, next_body, (jnp.int32(blocks),) * npairs)

    lanes = lax.broadcasted_iota(jnp.int32, counts_all.shape[1:], 1)
    sent_row = jnp.zeros(counts_all.shape[1:], jnp.int32)
    for o in peer_range:
        sent_row = jnp.where(lanes == o, sent[o], sent_row)
    counts_all[me] = sent_row

    unroll = divisor(cap, (8, 6, 4, 3, 2))

    def pack_for(pair):
        def body(i, k):
            for u in range(unroll):
                r = i * unroll + u
                row = den[jnp.minimum(k, blocks - 1)]
                for h in range(nrep):
                    pack[pair, h, r] = row[:, h * xq : (h + 1) * xq]
                k = next_smem[pair, jnp.minimum(k + 1, blocks)]
            return k

        lax.fori_loop(0, cap // unroll, body, next_smem[pair, 0])

    den_copy.wait()
    pack_for(pair_order[0])
    pl.semaphore_wait(barrier, greeted)

    def ints_copy(s, c, slot):
        return pltpu.make_async_remote_copy(
            src_ref=integrals_ref.at[pl.ds(c * step, step), :, quarter(s, rep)],
            dst_ref=ints.at[slot, pl.ds(c * step, step)],
            send_sem=ints_send.at[s, c],
            recv_sem=ints_recv.at[slot, c],
            device_id=device(me, s, rep),
            device_id_type=MESH,
        )

    def cnt_copy(pair, slot):
        return pltpu.make_async_remote_copy(
            src_ref=counts_all.at[me],
            dst_ref=counts_all.at[slot],
            send_sem=cnt_send.at[pair],
            recv_sem=cnt_recv.at[slot],
            device_id=device(pair, sub, rep),
            device_id_type=MESH,
        )

    def den_send_copy(pair, h, slot_pair, slot_rep):
        return pltpu.make_async_remote_copy(
            src_ref=pack.at[pair, h],
            dst_ref=arrived.at[slot_rep, pl.ds(slot_pair * cap, cap)],
            send_sem=den_send.at[pair, h],
            recv_sem=den_recv.at[slot_pair, slot_rep],
            device_id=device(pair, sub, h),
            device_id_type=MESH,
        )

    for pair in pair_peers:
        cnt_copy(pair, me).start()
    for i, pair in enumerate(pair_order):
        if i > 0:
            pack_for(pair)
        for h in [rep] + rep_peers:
            den_send_copy(pair, h, me, rep).start()
        if i == 0:
            for c in range(chunks):
                for s in sub_peers:
                    ints_copy(s, c, sub).start()
    pack_for(me)
    for h in rep_peers:
        den_send_copy(me, h, me, rep).start()
    own_den = pltpu.make_async_copy(
        pack.at[me, rep], arrived.at[rep, pl.ds(me * cap, cap)], local_sem
    )
    own_den.start()

    for pair in pair_peers:
        cnt_copy(pair, pair).wait_recv()
    to_smem = pltpu.make_async_copy(counts_all, counts_smem, den_send.at[me, rep])
    to_smem.start()
    to_smem.wait()
    starts = []
    finish = []
    total = jnp.int32(0)
    for s in range(npairs):
        starts.append(total)
        starts_smem[s] = total
        total = total + counts_smem[s, 0, me]
        finish.append(total)

    def place(j, carry):
        anchor = jnp.int32(0)
        start = jnp.int32(0)
        for s in range(npairs - 1):
            past = j >= finish[s]
            anchor = anchor + jnp.where(past, 1, 0)
            start = jnp.where(past, finish[s], start)
        places_smem[j] = jnp.minimum(anchor * cap + j - start, npairs * cap - 1)
        return carry

    lax.fori_loop(0, blocks, place, 0)

    own_den.wait()
    own_copy.wait()
    for h in rep_peers:
        den_send_copy(me, rep, me, h).wait_recv()
    for pair in reversed(pair_order):
        for h in [rep] + rep_peers:
            den_send_copy(pair, rep, pair, h).wait_recv()

    def block_ints(j):
        return jnp.concatenate([ints[s, j] for s in range(nsub)], axis=0)

    fit_unroll = divisor(step, (12, 8, 6, 4, 3, 2))
    fit = jnp.zeros(fit_pairs.shape[1:], jnp.float32)
    for c in range(chunks):
        for s in sub_peers:
            ints_copy(s, c, s).wait_recv()

        def fit_body(i, acc):
            for u in range(fit_unroll):
                j = c * step + i * fit_unroll + u
                at = places_smem[j]
                rows = jnp.concatenate([arrived[h, at] for h in range(nrep)], axis=0)
                acc = acc + lax.dot_general(
                    rows,
                    block_ints(j),
                    (((1,), (1,)), ((), ())),
                    preferred_element_type=jnp.float32,
                )
            return acc

        fit = lax.fori_loop(0, step // fit_unroll, fit_body, fit)

    plane_me = sub * nrep + rep
    fit_plane[plane_me] = fit

    def plane_copy(s, r, slot):
        return pltpu.make_async_remote_copy(
            src_ref=fit_plane.at[plane_me],
            dst_ref=fit_plane.at[slot],
            send_sem=plane_send.at[s * nrep + r],
            recv_sem=plane_recv.at[slot],
            device_id=device(me, s, r),
            device_id_type=MESH,
        )

    for s, r in reversed(plane_peers):
        plane_copy(s, r, plane_me).start()
    for s, r in plane_peers:
        plane_copy(s, r, s * nrep + r).wait_recv()
    fit = fit_plane[0]
    for i in range(1, nsub * nrep):
        fit = fit + fit_plane[i]
    fit_pairs[me] = fit

    def pairs_copy(pair, slot):
        return pltpu.make_async_remote_copy(
            src_ref=fit_pairs.at[me],
            dst_ref=fit_pairs.at[slot],
            send_sem=pairs_send.at[pair],
            recv_sem=pairs_recv.at[slot],
            device_id=device(pair, sub, rep),
            device_id_type=MESH,
        )

    for pair in pair_peers:
        pairs_copy(pair, me).start()
    for pair in pair_peers:
        pairs_copy(pair, pair).wait_recv()
    fit = fit_pairs[0]
    for i in range(1, npairs):
        fit = fit + fit_pairs[i]
    fitted = fit.astype(jnp.bfloat16)

    pieces = ret_send.shape[2]
    piece = cap // pieces
    piece_unroll = divisor(piece, (6, 4, 3, 2))

    def ret_copy(pair, h, part, slot_pair, slot_rep):
        return pltpu.make_async_remote_copy(
            src_ref=ret.at[pair, h, pl.ds(part * piece, piece)],
            dst_ref=homeward.at[slot_rep, pl.ds(slot_pair * cap + part * piece, piece)],
            send_sem=ret_send.at[pair, h, part],
            recv_sem=ret_recv.at[slot_pair, slot_rep, part],
            device_id=device(pair, sub, h),
            device_id_type=MESH,
        )

    def coulomb_for(pair, part):
        start = starts_smem[pair]

        def body(i, carry):
            for u in range(piece_unroll):
                r = part * piece + i * piece_unroll + u
                j = jnp.minimum(start + r, blocks - 1)
                rows = jnp.dot(
                    fitted, block_ints(j), preferred_element_type=jnp.float32
                ).astype(jnp.bfloat16)
                for h in range(nrep):
                    ret[pair, h, r] = rows[h * dens : (h + 1) * dens]
            return carry

        lax.fori_loop(0, piece // piece_unroll, body, 0)

    for pair in pair_order:
        for part in range(pieces):
            coulomb_for(pair, part)
            for h in [rep] + rep_peers:
                ret_copy(pair, h, part, me, rep).start()
    for part in range(pieces):
        coulomb_for(me, part)
        for h in rep_peers:
            ret_copy(me, h, part, me, rep).start()
    own_ret = pltpu.make_async_copy(
        ret.at[me, rep], homeward.at[rep, pl.ds(me * cap, cap)], local_sem
    )
    own_ret.start()

    for c in range(chunks):
        for s in sub_peers:
            ints_copy(s, c, sub).wait_send()
    for pair in pair_peers:
        cnt_copy(pair, me).wait_send()
        pairs_copy(pair, me).wait_send()
    for s, r in plane_peers:
        plane_copy(s, r, plane_me).wait_send()
    for pair in pair_peers:
        for h in [rep] + rep_peers:
            den_send_copy(pair, h, me, rep).wait_send()
    for h in rep_peers:
        den_send_copy(me, h, me, rep).wait_send()

    own_ret.wait()
    for part in range(pieces):
        for h in rep_peers:
            ret_copy(me, rep, part, me, h).wait_recv()
    for pair in reversed(pair_order):
        for part in range(pieces):
            for h in [rep] + rep_peers:
                ret_copy(pair, rep, part, pair, h).wait_recv()

    out_unroll = divisor(blocks, (8, 6, 4, 3, 2))

    def out_body(i, carry):
        for u in range(out_unroll):
            k = i * out_unroll + u
            at = out_ids_ref[k]
            out_ref[k] = jnp.concatenate([homeward[h, at] for h in range(nrep)], axis=1)
        return carry

    lax.fori_loop(0, blocks // out_unroll, out_body, 0)

    for part in range(pieces):
        for pair in pair_peers:
            for h in [rep] + rep_peers:
                ret_copy(pair, h, part, me, rep).wait_send()
        for h in rep_peers:
            ret_copy(me, h, part, me, rep).wait_send()


def on_device(integrals, density, block_owner):
    npairs = lax.axis_size("pairs")
    nsub = lax.axis_size("sub")
    nrep = lax.axis_size("rep")
    blocks, dens, width = density.shape
    p_dev = integrals.shape[1]
    xq = width // (nsub * nrep)
    cap = 2 * blocks // npairs
    chunks = divisor(blocks, (4, 3, 2))
    pieces = divisor(cap, (2,))
    vmem = pl.BlockSpec(memory_space=pltpu.VMEM)
    smem = pl.BlockSpec(memory_space=pltpu.SMEM)
    hbm = pl.BlockSpec(memory_space=pltpu.HBM)
    bf16 = jnp.bfloat16
    sems = pltpu.SemaphoreType.DMA
    rows = pl.pallas_call(
        functools.partial(exchange, npairs, nsub, nrep, chunks),
        out_shape=jax.ShapeDtypeStruct((blocks, dens, nrep * xq), bf16),
        in_specs=[smem, hbm, hbm],
        out_specs=vmem,
        scratch_shapes=[
            pltpu.VMEM((nsub, blocks, p_dev, xq), bf16),
            pltpu.VMEM((blocks, dens, nrep * xq), bf16),
            pltpu.VMEM((npairs, nrep, cap, dens, xq), bf16),
            pltpu.VMEM((nrep, npairs * cap, dens, xq), bf16),
            pltpu.VMEM((npairs, nrep, cap, dens, xq), bf16),
            pltpu.VMEM((nrep, npairs * cap, dens, xq), bf16),
            pltpu.SMEM((blocks,), jnp.int32),
            pltpu.SMEM((npairs, blocks + 1), jnp.int32),
            pltpu.VMEM((npairs, 8, 128), jnp.int32),
            pltpu.SMEM((npairs, 8, 128), jnp.int32),
            pltpu.SMEM((npairs,), jnp.int32),
            pltpu.SMEM((blocks,), jnp.int32),
            pltpu.VMEM((nsub * nrep, nrep * dens, nsub * p_dev), jnp.float32),
            pltpu.VMEM((npairs, nrep * dens, nsub * p_dev), jnp.float32),
            sems,
            sems,
            sems((nsub, chunks)),
            sems((nsub, chunks)),
            sems((npairs, nrep)),
            sems((npairs, nrep)),
            sems((npairs, nrep, pieces)),
            sems((npairs, nrep, pieces)),
            sems((npairs,)),
            sems((npairs,)),
            sems((nsub * nrep,)),
            sems((nsub * nrep,)),
            sems((npairs,)),
            sems((npairs,)),
        ],
        compiler_params=pltpu.CompilerParams(
            collective_id=0, has_side_effects=True, vmem_limit_bytes=105 * 512 * 1024
        ),
    )(block_owner, integrals, density)
    return rows.astype(jnp.float32)


def solution(mesh):
    in_specs = (
        P(("groups", "pairs"), "sub", None),
        P(("groups", "pairs"), "rep", None),
        P(("groups", "pairs")),
    )
    out_specs = P(("groups", "pairs"), "rep", "sub")
    return jax.shard_map(
        on_device, mesh=mesh, in_specs=in_specs, out_specs=out_specs, check_vma=False
    )
```

```python
import functools

import jax
import jax.numpy as jnp
from jax import lax
from jax.experimental import pallas as pl
from jax.experimental.pallas import tpu as pltpu
from jax.sharding import PartitionSpec as P

MESH = pl.DeviceIdType.MESH


def divisor(total, choices):
    for c in choices:
        if total % c == 0:
            return c
    return 1


def exchange(
    npairs,
    nsub,
    nrep,
    chunks,
    owner_ref,
    integrals_ref,
    density_ref,
    out_ref,
    ints,
    den,
    pack,
    arrived,
    ret,
    homeward,
    out_ids_ref,
    next_smem,
    counts_all,
    counts_smem,
    starts_smem,
    places_smem,
    fit_plane,
    fit_pairs,
    local_sem,
    own_sem,
    ints_send,
    ints_recv,
    den_send,
    den_recv,
    ret_send,
    ret_recv,
    cnt_send,
    cnt_recv,
    plane_send,
    plane_recv,
    pairs_send,
    pairs_recv,
):
    me = lax.axis_index("pairs")
    sub = lax.axis_index("sub")
    rep = lax.axis_index("rep")
    blocks, dens, _ = density_ref.shape
    xq = ints.shape[3]
    cap = arrived.shape[1] // npairs
    step = blocks // chunks

    def device(pair, s, r):
        return {"pairs": pair, "sub": s, "rep": r}

    def quarter(s, r):
        return pl.ds(pl.multiple_of((s * nrep + r) * xq, 128), xq)

    den_copy = pltpu.make_async_copy(
        density_ref.at[:, :, pl.ds(pl.multiple_of(sub * (nrep * xq), 128), nrep * xq)],
        den,
        local_sem,
    )
    den_copy.start()
    own_copy = pltpu.make_async_copy(
        integrals_ref.at[:, :, quarter(sub, rep)], ints.at[sub], own_sem
    )
    own_copy.start()

    pair_order = [lax.rem(me + npairs // 2 + i, npairs) for i in range(npairs - npairs // 2)] + [
        lax.rem(me + i, npairs) for i in range(1, npairs // 2)
    ]
    pair_peers = pair_order
    sub_peers = [lax.rem(sub + i, nsub) for i in range(1, nsub)]
    rep_peers = [lax.rem(rep + i, nrep) for i in range(1, nrep)]
    plane_peers = (
        [(sub, r) for r in rep_peers]
        + [(s, rep) for s in sub_peers]
        + [(s, r) for s in sub_peers for r in rep_peers]
    )

    barrier = pltpu.get_barrier_semaphore()
    greeted = 0
    for pair in pair_peers:
        for r in [rep] + rep_peers:
            pl.semaphore_signal(
                barrier, inc=1, device_id=device(pair, sub, r), device_id_type=MESH
            )
            greeted += 1
    for s, r in plane_peers:
        pl.semaphore_signal(barrier, inc=1, device_id=device(me, s, r), device_id_type=MESH)
        greeted += 1

    peer_range = range(npairs)

    def rank_body(k, seen):
        owner = owner_ref[k]
        at = owner * cap
        after = []
        for o in peer_range:
            mine = owner == o
            at = at + jnp.where(mine, seen[o], 0)
            after.append(seen[o] + jnp.where(mine, 1, 0))
        out_ids_ref[k] = at
        return tuple(after)

    sent = lax.fori_loop(0, blocks, rank_body, (jnp.int32(0),) * npairs)

    for o in peer_range:
        next_smem[o, blocks] = jnp.int32(blocks)

    def next_body(i, following):
        k = blocks - 1 - i
        owner = owner_ref[k]
        found = []
        for o in peer_range:
            found.append(jnp.where(owner == o, k, following[o]))
            next_smem[o, k] = found[o]
        return tuple(found)

    lax.fori_loop(0, blocks, next_body, (jnp.int32(blocks),) * npairs)

    lanes = lax.broadcasted_iota(jnp.int32, counts_all.shape[1:], 1)
    sent_row = jnp.zeros(counts_all.shape[1:], jnp.int32)
    for o in peer_range:
        sent_row = jnp.where(lanes == o, sent[o], sent_row)
    counts_all[me] = sent_row

    unroll = divisor(cap, (8, 6, 4, 3, 2))

    def pack_for(pair):
        def body(i, k):
            for u in range(unroll):
                r = i * unroll + u
                row = den[jnp.minimum(k, blocks - 1)]
                for h in range(nrep):
                    pack[pair, h, r] = row[:, h * xq : (h + 1) * xq]
                k = next_smem[pair, jnp.minimum(k + 1, blocks)]
            return k

        lax.fori_loop(0, cap // unroll, body, next_smem[pair, 0])

    pl.semaphore_wait(barrier, greeted)

    def ints_copy(s, c, slot):
        return pltpu.make_async_remote_copy(
            src_ref=integrals_ref.at[pl.ds(c * step, step), :, quarter(s, rep)],
            dst_ref=ints.at[slot, pl.ds(c * step, step)],
            send_sem=ints_send.at[s, c],
            recv_sem=ints_recv.at[slot, c],
            device_id=device(me, s, rep),
            device_id_type=MESH,
        )

    def cnt_copy(pair, slot):
        return pltpu.make_async_remote_copy(
            src_ref=counts_all.at[me],
            dst_ref=counts_all.at[slot],
            send_sem=cnt_send.at[pair],
            recv_sem=cnt_recv.at[slot],
            device_id=device(pair, sub, rep),
            device_id_type=MESH,
        )

    def den_send_copy(pair, h, slot_pair, slot_rep):
        return pltpu.make_async_remote_copy(
            src_ref=pack.at[pair, h],
            dst_ref=arrived.at[slot_rep, pl.ds(slot_pair * cap, cap)],
            send_sem=den_send.at[pair, h],
            recv_sem=den_recv.at[slot_pair, slot_rep],
            device_id=device(pair, sub, h),
            device_id_type=MESH,
        )

    for pair in pair_peers:
        cnt_copy(pair, me).start()
    for c in range(chunks):
        for s in sub_peers:
            ints_copy(s, c, sub).start()
    den_copy.wait()
    for pair in pair_order:
        pack_for(pair)
        for h in [rep] + rep_peers:
            den_send_copy(pair, h, me, rep).start()
    pack_for(me)
    for h in rep_peers:
        den_send_copy(me, h, me, rep).start()
    own_den = pltpu.make_async_copy(
        pack.at[me, rep], arrived.at[rep, pl.ds(me * cap, cap)], local_sem
    )
    own_den.start()

    for pair in pair_peers:
        cnt_copy(pair, pair).wait_recv()
    to_smem = pltpu.make_async_copy(counts_all, counts_smem, den_send.at[me, rep])
    to_smem.start()
    to_smem.wait()
    starts = []
    finish = []
    total = jnp.int32(0)
    for s in range(npairs):
        starts.append(total)
        starts_smem[s] = total
        total = total + counts_smem[s, 0, me]
        finish.append(total)

    def place(j, carry):
        anchor = jnp.int32(0)
        start = jnp.int32(0)
        for s in range(npairs - 1):
            past = j >= finish[s]
            anchor = anchor + jnp.where(past, 1, 0)
            start = jnp.where(past, finish[s], start)
        places_smem[j] = jnp.minimum(anchor * cap + j - start, npairs * cap - 1)
        return carry

    lax.fori_loop(0, blocks, place, 0)

    own_den.wait()
    own_copy.wait()
    for h in rep_peers:
        den_send_copy(me, rep, me, h).wait_recv()
    for pair in reversed(pair_order):
        for h in [rep] + rep_peers:
            den_send_copy(pair, rep, pair, h).wait_recv()

    def block_ints(j):
        return jnp.concatenate([ints[s, j] for s in range(nsub)], axis=0)

    fit_unroll = divisor(step, (12, 8, 6, 4, 3, 2))
    fit = jnp.zeros(fit_pairs.shape[1:], jnp.float32)
    for c in range(chunks):
        for s in sub_peers:
            ints_copy(s, c, s).wait_recv()

        def fit_body(i, acc):
            for u in range(fit_unroll):
                j = c * step + i * fit_unroll + u
                at = places_smem[j]
                rows = jnp.concatenate([arrived[h, at] for h in range(nrep)], axis=0)
                acc = acc + lax.dot_general(
                    rows,
                    block_ints(j),
                    (((1,), (1,)), ((), ())),
                    preferred_element_type=jnp.float32,
                )
            return acc

        fit = lax.fori_loop(0, step // fit_unroll, fit_body, fit)

    plane_me = sub * nrep + rep
    fit_plane[plane_me] = fit

    def plane_copy(s, r, slot):
        return pltpu.make_async_remote_copy(
            src_ref=fit_plane.at[plane_me],
            dst_ref=fit_plane.at[slot],
            send_sem=plane_send.at[s * nrep + r],
            recv_sem=plane_recv.at[slot],
            device_id=device(me, s, r),
            device_id_type=MESH,
        )

    for s, r in reversed(plane_peers):
        plane_copy(s, r, plane_me).start()
    for s, r in plane_peers:
        plane_copy(s, r, s * nrep + r).wait_recv()
    fit = fit_plane[0]
    for i in range(1, nsub * nrep):
        fit = fit + fit_plane[i]
    fit_pairs[me] = fit

    def pairs_copy(pair, slot):
        return pltpu.make_async_remote_copy(
            src_ref=fit_pairs.at[me],
            dst_ref=fit_pairs.at[slot],
            send_sem=pairs_send.at[pair],
            recv_sem=pairs_recv.at[slot],
            device_id=device(pair, sub, rep),
            device_id_type=MESH,
        )

    for pair in pair_peers:
        pairs_copy(pair, me).start()
    for pair in pair_peers:
        pairs_copy(pair, pair).wait_recv()
    fit = fit_pairs[0]
    for i in range(1, npairs):
        fit = fit + fit_pairs[i]
    fitted = fit.astype(jnp.bfloat16)

    pieces = ret_send.shape[2]
    piece = cap // pieces
    piece_unroll = divisor(piece, (6, 4, 3, 2))

    def ret_copy(pair, h, part, slot_pair, slot_rep):
        return pltpu.make_async_remote_copy(
            src_ref=ret.at[pair, h, pl.ds(part * piece, piece)],
            dst_ref=homeward.at[slot_rep, pl.ds(slot_pair * cap + part * piece, piece)],
            send_sem=ret_send.at[pair, h, part],
            recv_sem=ret_recv.at[slot_pair, slot_rep, part],
            device_id=device(pair, sub, h),
            device_id_type=MESH,
        )

    def coulomb_for(pair, part):
        start = starts_smem[pair]

        def body(i, carry):
            for u in range(piece_unroll):
                r = part * piece + i * piece_unroll + u
                j = jnp.minimum(start + r, blocks - 1)
                rows = jnp.dot(
                    fitted, block_ints(j), preferred_element_type=jnp.float32
                ).astype(jnp.bfloat16)
                for h in range(nrep):
                    ret[pair, h, r] = rows[h * dens : (h + 1) * dens]
            return carry

        lax.fori_loop(0, piece // piece_unroll, body, 0)

    for pair in pair_order:
        for part in range(pieces):
            coulomb_for(pair, part)
            for h in [rep] + rep_peers:
                ret_copy(pair, h, part, me, rep).start()
    for part in range(pieces):
        coulomb_for(me, part)
        for h in rep_peers:
            ret_copy(me, h, part, me, rep).start()
    own_ret = pltpu.make_async_copy(
        ret.at[me, rep], homeward.at[rep, pl.ds(me * cap, cap)], local_sem
    )
    own_ret.start()

    for c in range(chunks):
        for s in sub_peers:
            ints_copy(s, c, sub).wait_send()
    for pair in pair_peers:
        cnt_copy(pair, me).wait_send()
        pairs_copy(pair, me).wait_send()
    for s, r in plane_peers:
        plane_copy(s, r, plane_me).wait_send()
    for pair in pair_peers:
        for h in [rep] + rep_peers:
            den_send_copy(pair, h, me, rep).wait_send()
    for h in rep_peers:
        den_send_copy(me, h, me, rep).wait_send()

    own_ret.wait()
    for part in range(pieces):
        for h in rep_peers:
            ret_copy(me, rep, part, me, h).wait_recv()
    for pair in reversed(pair_order):
        for part in range(pieces):
            for h in [rep] + rep_peers:
                ret_copy(pair, rep, part, pair, h).wait_recv()

    out_unroll = divisor(blocks, (8, 6, 4, 3, 2))

    def out_body(i, carry):
        for u in range(out_unroll):
            k = i * out_unroll + u
            at = out_ids_ref[k]
            out_ref[k] = jnp.concatenate([homeward[h, at] for h in range(nrep)], axis=1)
        return carry

    lax.fori_loop(0, blocks // out_unroll, out_body, 0)

    for part in range(pieces):
        for pair in pair_peers:
            for h in [rep] + rep_peers:
                ret_copy(pair, h, part, me, rep).wait_send()
        for h in rep_peers:
            ret_copy(me, h, part, me, rep).wait_send()


def on_device(integrals, density, block_owner):
    npairs = lax.axis_size("pairs")
    nsub = lax.axis_size("sub")
    nrep = lax.axis_size("rep")
    blocks, dens, width = density.shape
    p_dev = integrals.shape[1]
    xq = width // (nsub * nrep)
    cap = 2 * blocks // npairs
    chunks = divisor(blocks, (4, 3, 2))
    pieces = divisor(cap, (2,))
    vmem = pl.BlockSpec(memory_space=pltpu.VMEM)
    smem = pl.BlockSpec(memory_space=pltpu.SMEM)
    hbm = pl.BlockSpec(memory_space=pltpu.HBM)
    bf16 = jnp.bfloat16
    sems = pltpu.SemaphoreType.DMA
    rows = pl.pallas_call(
        functools.partial(exchange, npairs, nsub, nrep, chunks),
        out_shape=jax.ShapeDtypeStruct((blocks, dens, nrep * xq), bf16),
        in_specs=[smem, hbm, hbm],
        out_specs=vmem,
        scratch_shapes=[
            pltpu.VMEM((nsub, blocks, p_dev, xq), bf16),
            pltpu.VMEM((blocks, dens, nrep * xq), bf16),
            pltpu.VMEM((npairs, nrep, cap, dens, xq), bf16),
            pltpu.VMEM((nrep, npairs * cap, dens, xq), bf16),
            pltpu.VMEM((npairs, nrep, cap, dens, xq), bf16),
            pltpu.VMEM((nrep, npairs * cap, dens, xq), bf16),
            pltpu.SMEM((blocks,), jnp.int32),
            pltpu.SMEM((npairs, blocks + 1), jnp.int32),
            pltpu.VMEM((npairs, 8, 128), jnp.int32),
            pltpu.SMEM((npairs, 8, 128), jnp.int32),
            pltpu.SMEM((npairs,), jnp.int32),
            pltpu.SMEM((blocks,), jnp.int32),
            pltpu.VMEM((nsub * nrep, nrep * dens, nsub * p_dev), jnp.float32),
            pltpu.VMEM((npairs, nrep * dens, nsub * p_dev), jnp.float32),
            sems,
            sems,
            sems((nsub, chunks)),
            sems((nsub, chunks)),
            sems((npairs, nrep)),
            sems((npairs, nrep)),
            sems((npairs, nrep, pieces)),
            sems((npairs, nrep, pieces)),
            sems((npairs,)),
            sems((npairs,)),
            sems((nsub * nrep,)),
            sems((nsub * nrep,)),
            sems((npairs,)),
            sems((npairs,)),
        ],
        compiler_params=pltpu.CompilerParams(
            collective_id=0, has_side_effects=True, vmem_limit_bytes=105 * 512 * 1024
        ),
    )(block_owner, integrals, density)
    return rows.astype(jnp.float32)


def solution(mesh):
    in_specs = (
        P(("groups", "pairs"), "sub", None),
        P(("groups", "pairs"), "rep", None),
        P(("groups", "pairs")),
    )
    out_specs = P(("groups", "pairs"), "rep", "sub")
    return jax.shard_map(
        on_device, mesh=mesh, in_specs=in_specs, out_specs=out_specs, check_vma=False
    )
```

```python
import functools

import jax
import jax.numpy as jnp
from jax import lax
from jax.experimental import pallas as pl
from jax.experimental.pallas import tpu as pltpu
from jax.sharding import PartitionSpec as P

MESH = pl.DeviceIdType.MESH


def divisor(total, choices):
    for c in choices:
        if total % c == 0:
            return c
    return 1


def exchange(
    npairs,
    nsub,
    nrep,
    chunks,
    owner_ref,
    integrals_ref,
    density_ref,
    out_ref,
    ints,
    den,
    pack,
    arrived,
    ret,
    homeward,
    out_ids_ref,
    next_smem,
    counts_all,
    counts_smem,
    starts_smem,
    places_smem,
    fit_plane,
    fit_pairs,
    local_sem,
    own_sem,
    ints_send,
    ints_recv,
    den_send,
    den_recv,
    ret_send,
    ret_recv,
    cnt_send,
    cnt_recv,
    plane_send,
    plane_recv,
    pairs_send,
    pairs_recv,
):
    me = lax.axis_index("pairs")
    sub = lax.axis_index("sub")
    rep = lax.axis_index("rep")
    blocks, dens, _ = density_ref.shape
    xq = ints.shape[3]
    cap = arrived.shape[1] // npairs
    step = blocks // chunks

    def device(pair, s, r):
        return {"pairs": pair, "sub": s, "rep": r}

    def quarter(s, r):
        return pl.ds(pl.multiple_of((s * nrep + r) * xq, 128), xq)

    den_copy = pltpu.make_async_copy(
        density_ref.at[:, :, pl.ds(pl.multiple_of(sub * (nrep * xq), 128), nrep * xq)],
        den,
        local_sem,
    )
    den_copy.start()
    own_copy = pltpu.make_async_copy(
        integrals_ref.at[:, :, quarter(sub, rep)], ints.at[sub], own_sem
    )
    own_copy.start()

    pair_order = [lax.rem(me + npairs // 2 + i, npairs) for i in range(npairs - npairs // 2)] + [
        lax.rem(me + i, npairs) for i in range(1, npairs // 2)
    ]
    pair_peers = pair_order
    sub_peers = [lax.rem(sub + i, nsub) for i in range(1, nsub)]
    rep_peers = [lax.rem(rep + i, nrep) for i in range(1, nrep)]
    plane_peers = (
        [(sub, r) for r in rep_peers]
        + [(s, rep) for s in sub_peers]
        + [(s, r) for s in sub_peers for r in rep_peers]
    )

    barrier = pltpu.get_barrier_semaphore()
    greeted = 0
    for pair in pair_peers:
        for r in [rep] + rep_peers:
            pl.semaphore_signal(
                barrier, inc=1, device_id=device(pair, sub, r), device_id_type=MESH
            )
            greeted += 1
    for s, r in plane_peers:
        pl.semaphore_signal(barrier, inc=1, device_id=device(me, s, r), device_id_type=MESH)
        greeted += 1

    peer_range = range(npairs)

    def rank_body(k, seen):
        owner = owner_ref[k]
        at = owner * cap
        after = []
        for o in peer_range:
            mine = owner == o
            at = at + jnp.where(mine, seen[o], 0)
            after.append(seen[o] + jnp.where(mine, 1, 0))
        out_ids_ref[k] = at
        return tuple(after)

    sent = lax.fori_loop(0, blocks, rank_body, (jnp.int32(0),) * npairs)

    for o in peer_range:
        next_smem[o, blocks] = jnp.int32(blocks)

    def next_body(i, following):
        k = blocks - 1 - i
        owner = owner_ref[k]
        found = []
        for o in peer_range:
            found.append(jnp.where(owner == o, k, following[o]))
            next_smem[o, k] = found[o]
        return tuple(found)

    lax.fori_loop(0, blocks, next_body, (jnp.int32(blocks),) * npairs)

    lanes = lax.broadcasted_iota(jnp.int32, counts_all.shape[1:], 1)
    sent_row = jnp.zeros(counts_all.shape[1:], jnp.int32)
    for o in peer_range:
        sent_row = jnp.where(lanes == o, sent[o], sent_row)
    counts_all[me] = sent_row

    unroll = divisor(cap, (8, 6, 4, 3, 2))

    def pack_for(pair):
        def body(i, k):
            for u in range(unroll):
                r = i * unroll + u
                row = den[jnp.minimum(k, blocks - 1)]
                for h in range(nrep):
                    pack[pair, h, r] = row[:, h * xq : (h + 1) * xq]
                k = next_smem[pair, jnp.minimum(k + 1, blocks)]
            return k

        lax.fori_loop(0, cap // unroll, body, next_smem[pair, 0])

    pl.semaphore_wait(barrier, greeted)

    def ints_copy(s, c, slot):
        return pltpu.make_async_remote_copy(
            src_ref=integrals_ref.at[pl.ds(c * step, step), :, quarter(s, rep)],
            dst_ref=ints.at[slot, pl.ds(c * step, step)],
            send_sem=ints_send.at[s, c],
            recv_sem=ints_recv.at[slot, c],
            device_id=device(me, s, rep),
            device_id_type=MESH,
        )

    def cnt_copy(pair, slot):
        return pltpu.make_async_remote_copy(
            src_ref=counts_all.at[me],
            dst_ref=counts_all.at[slot],
            send_sem=cnt_send.at[pair],
            recv_sem=cnt_recv.at[slot],
            device_id=device(pair, sub, rep),
            device_id_type=MESH,
        )

    def den_send_copy(pair, h, slot_pair, slot_rep):
        return pltpu.make_async_remote_copy(
            src_ref=pack.at[pair, h],
            dst_ref=arrived.at[slot_rep, pl.ds(slot_pair * cap, cap)],
            send_sem=den_send.at[pair, h],
            recv_sem=den_recv.at[slot_pair, slot_rep],
            device_id=device(pair, sub, h),
            device_id_type=MESH,
        )

    for pair in pair_peers:
        cnt_copy(pair, me).start()
    for c in range(chunks):
        for s in sub_peers:
            ints_copy(s, c, sub).start()
    den_copy.wait()
    for pair in pair_order:
        pack_for(pair)
        for h in [rep] + rep_peers:
            den_send_copy(pair, h, me, rep).start()
    pack_for(me)
    for h in rep_peers:
        den_send_copy(me, h, me, rep).start()
    own_den = pltpu.make_async_copy(
        pack.at[me, rep], arrived.at[rep, pl.ds(me * cap, cap)], local_sem
    )
    own_den.start()

    for pair in pair_peers:
        cnt_copy(pair, pair).wait_recv()
    to_smem = pltpu.make_async_copy(counts_all, counts_smem, den_send.at[me, rep])
    to_smem.start()
    to_smem.wait()
    starts = []
    finish = []
    total = jnp.int32(0)
    for s in range(npairs):
        starts.append(total)
        starts_smem[s] = total
        total = total + counts_smem[s, 0, me]
        finish.append(total)

    def place(j, carry):
        anchor = jnp.int32(0)
        start = jnp.int32(0)
        for s in range(npairs - 1):
            past = j >= finish[s]
            anchor = anchor + jnp.where(past, 1, 0)
            start = jnp.where(past, finish[s], start)
        places_smem[j] = jnp.minimum(anchor * cap + j - start, npairs * cap - 1)
        return carry

    lax.fori_loop(0, blocks, place, 0)

    own_den.wait()
    own_copy.wait()
    for h in rep_peers:
        den_send_copy(me, rep, me, h).wait_recv()
    for pair in reversed(pair_order):
        for h in [rep] + rep_peers:
            den_send_copy(pair, rep, pair, h).wait_recv()

    def block_ints(j):
        return jnp.concatenate([ints[s, j] for s in range(nsub)], axis=0)

    fit_unroll = divisor(step, (12, 8, 6, 4, 3, 2))
    fit = jnp.zeros(fit_pairs.shape[1:], jnp.float32)
    for c in range(chunks):
        for s in sub_peers:
            ints_copy(s, c, s).wait_recv()

        def fit_body(i, acc):
            for u in range(fit_unroll):
                j = c * step + i * fit_unroll + u
                at = places_smem[j]
                rows = jnp.concatenate([arrived[h, at] for h in range(nrep)], axis=0)
                acc = acc + lax.dot_general(
                    rows,
                    block_ints(j),
                    (((1,), (1,)), ((), ())),
                    preferred_element_type=jnp.float32,
                )
            return acc

        fit = lax.fori_loop(0, step // fit_unroll, fit_body, fit)

    fit_pairs[me] = fit

    def pairs_copy(pair, slot):
        return pltpu.make_async_remote_copy(
            src_ref=fit_pairs.at[me],
            dst_ref=fit_pairs.at[slot],
            send_sem=pairs_send.at[pair],
            recv_sem=pairs_recv.at[slot],
            device_id=device(pair, sub, rep),
            device_id_type=MESH,
        )

    for pair in pair_peers:
        pairs_copy(pair, me).start()
    for pair in pair_peers:
        pairs_copy(pair, pair).wait_recv()
    fit = fit_pairs[0]
    for i in range(1, npairs):
        fit = fit + fit_pairs[i]

    plane_me = sub * nrep + rep
    fit_plane[plane_me] = fit

    def plane_copy(s, r, slot):
        return pltpu.make_async_remote_copy(
            src_ref=fit_plane.at[plane_me],
            dst_ref=fit_plane.at[slot],
            send_sem=plane_send.at[s * nrep + r],
            recv_sem=plane_recv.at[slot],
            device_id=device(me, s, r),
            device_id_type=MESH,
        )

    for s, r in reversed(plane_peers):
        plane_copy(s, r, plane_me).start()
    for s, r in plane_peers:
        plane_copy(s, r, s * nrep + r).wait_recv()
    fit = fit_plane[0]
    for i in range(1, nsub * nrep):
        fit = fit + fit_plane[i]
    fitted = fit.astype(jnp.bfloat16)

    pieces = ret_send.shape[2]
    piece = cap // pieces
    piece_unroll = divisor(piece, (6, 4, 3, 2))

    def ret_copy(pair, h, part, slot_pair, slot_rep):
        return pltpu.make_async_remote_copy(
            src_ref=ret.at[pair, h, pl.ds(part * piece, piece)],
            dst_ref=homeward.at[slot_rep, pl.ds(slot_pair * cap + part * piece, piece)],
            send_sem=ret_send.at[pair, h, part],
            recv_sem=ret_recv.at[slot_pair, slot_rep, part],
            device_id=device(pair, sub, h),
            device_id_type=MESH,
        )

    def coulomb_for(pair, part):
        start = starts_smem[pair]

        def body(i, carry):
            for u in range(piece_unroll):
                r = part * piece + i * piece_unroll + u
                j = jnp.minimum(start + r, blocks - 1)
                rows = jnp.dot(
                    fitted, block_ints(j), preferred_element_type=jnp.float32
                ).astype(jnp.bfloat16)
                for h in range(nrep):
                    ret[pair, h, r] = rows[h * dens : (h + 1) * dens]
            return carry

        lax.fori_loop(0, piece // piece_unroll, body, 0)

    for pair in pair_order:
        for part in range(pieces):
            coulomb_for(pair, part)
            for h in [rep] + rep_peers:
                ret_copy(pair, h, part, me, rep).start()
    for part in range(pieces):
        coulomb_for(me, part)
        for h in rep_peers:
            ret_copy(me, h, part, me, rep).start()
    own_ret = pltpu.make_async_copy(
        ret.at[me, rep], homeward.at[rep, pl.ds(me * cap, cap)], local_sem
    )
    own_ret.start()

    for c in range(chunks):
        for s in sub_peers:
            ints_copy(s, c, sub).wait_send()
    for pair in pair_peers:
        cnt_copy(pair, me).wait_send()
        pairs_copy(pair, me).wait_send()
    for s, r in plane_peers:
        plane_copy(s, r, plane_me).wait_send()
    for pair in pair_peers:
        for h in [rep] + rep_peers:
            den_send_copy(pair, h, me, rep).wait_send()
    for h in rep_peers:
        den_send_copy(me, h, me, rep).wait_send()

    own_ret.wait()
    for part in range(pieces):
        for h in rep_peers:
            ret_copy(me, rep, part, me, h).wait_recv()
    for pair in reversed(pair_order):
        for part in range(pieces):
            for h in [rep] + rep_peers:
                ret_copy(pair, rep, part, pair, h).wait_recv()

    out_unroll = divisor(blocks, (8, 6, 4, 3, 2))

    def out_body(i, carry):
        for u in range(out_unroll):
            k = i * out_unroll + u
            at = out_ids_ref[k]
            out_ref[k] = jnp.concatenate([homeward[h, at] for h in range(nrep)], axis=1)
        return carry

    lax.fori_loop(0, blocks // out_unroll, out_body, 0)

    for part in range(pieces):
        for pair in pair_peers:
            for h in [rep] + rep_peers:
                ret_copy(pair, h, part, me, rep).wait_send()
        for h in rep_peers:
            ret_copy(me, h, part, me, rep).wait_send()


def on_device(integrals, density, block_owner):
    npairs = lax.axis_size("pairs")
    nsub = lax.axis_size("sub")
    nrep = lax.axis_size("rep")
    blocks, dens, width = density.shape
    p_dev = integrals.shape[1]
    xq = width // (nsub * nrep)
    cap = 2 * blocks // npairs
    chunks = divisor(blocks, (4, 3, 2))
    pieces = divisor(cap, (2,))
    vmem = pl.BlockSpec(memory_space=pltpu.VMEM)
    smem = pl.BlockSpec(memory_space=pltpu.SMEM)
    hbm = pl.BlockSpec(memory_space=pltpu.HBM)
    bf16 = jnp.bfloat16
    sems = pltpu.SemaphoreType.DMA
    rows = pl.pallas_call(
        functools.partial(exchange, npairs, nsub, nrep, chunks),
        out_shape=jax.ShapeDtypeStruct((blocks, dens, nrep * xq), bf16),
        in_specs=[smem, hbm, hbm],
        out_specs=vmem,
        scratch_shapes=[
            pltpu.VMEM((nsub, blocks, p_dev, xq), bf16),
            pltpu.VMEM((blocks, dens, nrep * xq), bf16),
            pltpu.VMEM((npairs, nrep, cap, dens, xq), bf16),
            pltpu.VMEM((nrep, npairs * cap, dens, xq), bf16),
            pltpu.VMEM((npairs, nrep, cap, dens, xq), bf16),
            pltpu.VMEM((nrep, npairs * cap, dens, xq), bf16),
            pltpu.SMEM((blocks,), jnp.int32),
            pltpu.SMEM((npairs, blocks + 1), jnp.int32),
            pltpu.VMEM((npairs, 8, 128), jnp.int32),
            pltpu.SMEM((npairs, 8, 128), jnp.int32),
            pltpu.SMEM((npairs,), jnp.int32),
            pltpu.SMEM((blocks,), jnp.int32),
            pltpu.VMEM((nsub * nrep, nrep * dens, nsub * p_dev), jnp.float32),
            pltpu.VMEM((npairs, nrep * dens, nsub * p_dev), jnp.float32),
            sems,
            sems,
            sems((nsub, chunks)),
            sems((nsub, chunks)),
            sems((npairs, nrep)),
            sems((npairs, nrep)),
            sems((npairs, nrep, pieces)),
            sems((npairs, nrep, pieces)),
            sems((npairs,)),
            sems((npairs,)),
            sems((nsub * nrep,)),
            sems((nsub * nrep,)),
            sems((npairs,)),
            sems((npairs,)),
        ],
        compiler_params=pltpu.CompilerParams(
            collective_id=0, has_side_effects=True, vmem_limit_bytes=105 * 512 * 1024
        ),
    )(block_owner, integrals, density)
    return rows.astype(jnp.float32)


def solution(mesh):
    in_specs = (
        P(("groups", "pairs"), "sub", None),
        P(("groups", "pairs"), "rep", None),
        P(("groups", "pairs")),
    )
    out_specs = P(("groups", "pairs"), "rep", "sub")
    return jax.shard_map(
        on_device, mesh=mesh, in_specs=in_specs, out_specs=out_specs, check_vma=False
    )
```
